32 devices in a mesh: groups: 2 (over x), ctx: 16 (over z, y, core).
Axes of the slice: x: 2, y: 2, z: 4, core: 2. Of those that a mesh axis runs over, the one named last changes fastest.
Arguments:
- conv_input: bfloat16 [4096, 2176], P(('groups', 'ctx')), parts along dimension 0, may hold values from -6 to 6
- conv_weight: float32 [4, 2176], replicated, may hold values from -3 to 3
- log_decay: float32 [32, 4096], P(None, ('groups', 'ctx')), parts along dimension 1, may hold values from -6 to 0
- level_weight: float32 [12, 32, 4096], P(None, None, ('groups', 'ctx')), parts along dimension 2, may hold values from 0.5 to 2
- grad_out: bfloat16 [4096, 2048], P(('groups', 'ctx')), parts along dimension 0, may hold values from -1.5 to 1.5
Outputs:
- mixed: bfloat16 [4096, 2048], P(('groups', 'ctx')), parts along dimension 0
- grad_input: bfloat16 [4096, 2176], P(('groups', 'ctx')), parts along dimension 0
- grad_level: float32 [12, 32, 4096], P(None, None, ('groups', 'ctx')), parts along dimension 2
- grad_conv: float32 [8, 2176], P('groups'), parts along dimension 0
The draws below stay inside these ranges and needn't reach their ends.
There are 2 independent parts, one for each index of `groups`. The reference program is written for one: setup_inputs(seed, part) draws one part's arguments, and reference() takes and returns one part's arrays. A program takes and returns all parts, laid end to end along the dimension named above; an argument that names none is the same for every part. Nothing has to cross between parts.
All inputs are finite; a program needn't handle non-finite values.
Results may differ from the reference program's by a relative error of at most 0.005.
Values may be sent and summed in bfloat16 or wider, within the bound.
A program may use at most 128 MiB of HBM per device.

```python
import math
import jax
import jax.numpy as jnp
from jax import lax

HEADS = 32
BLOCK = 64
CONV = 4
LEVELS = 12
TOK_DEV = 128
TOKEN_COUNT = 2048
WIDTH = 2048
CONV_CH = 2176
N_CTX = 16


def draw_log_decay(key, part):
    key = jax.random.fold_in(key, 7)
    random_subkey_list = jax.random.split(key, 7)
    slow_share = 0.5
    is_slow = jax.random.uniform(random_subkey_list[0], (HEADS,)) < slow_share
    slow_rate = jax.random.uniform(random_subkey_list[1], (HEADS,), minval=0.1, maxval=1.5) / TOKEN_COUNT
    fast_rate = jax.random.uniform(random_subkey_list[2], (HEADS,), minval=0.02, maxval=0.05)
    decay_speed = jnp.where(is_slow, slow_rate, fast_rate)
    segment_count = TOKEN_COUNT // TOK_DEV
    segment_multiplier = jnp.exp(jax.random.uniform(random_subkey_list[3], (HEADS, segment_count), minval=-0.7, maxval=0.7))
    segment_multiplier = jnp.repeat(segment_multiplier, TOK_DEV, axis=1)
    token_multiplier = jnp.exp(jax.random.uniform(random_subkey_list[4], (HEADS, TOKEN_COUNT), minval=-0.35, maxval=0.35))
    spike_position = jax.random.randint(random_subkey_list[5], (8,), 0, TOKEN_COUNT)
    spike_level = jax.random.uniform(random_subkey_list[6], (8,), minval=0.22, maxval=0.69)
    spike_token_rows = jnp.sum(jnp.where(jnp.arange(TOKEN_COUNT)[None, :] == spike_position[:, None], spike_level[:, None], 0.0), axis=0)
    return -(decay_speed[:, None] * segment_multiplier * token_multiplier) - spike_token_rows[None, :]


def steps_of(rng, shape, cuts, low, high):
    def one(axis_at, blocks):
        draws = jax.random.uniform(jax.random.fold_in(jax.random.fold_in(rng, 6), axis_at), (blocks,), jnp.float32, low / len(cuts), high / len(cuts))
        return jnp.repeat(jnp.exp(draws), shape[axis_at] // blocks).reshape((-1,) + (1,) * (len(shape) - axis_at - 1))

    factor_of = one(*cuts[0])
    for cut in cuts[1:]:
        factor_of = factor_of * one(*cut)
    return factor_of


def normal_values(stream_key, extent, scale, reach, cuts=(), kind=jnp.bfloat16):
    entries = jax.random.normal(stream_key, extent, jnp.float32) * scale
    if len(cuts) > 0:
        entries = steps_of(stream_key, extent, cuts, -0.22, 0.18) * entries
    return jnp.clip(entries, min=-reach, max=reach).astype(kind)


def setup_inputs(seed: int = 0, part: int = 0) -> dict:
    keys = jax.random.split(jax.random.key(seed), 6)
    part_splits = jax.random.split(jax.random.fold_in(keys[5], part), 6)
    return {
        "conv_input": normal_values(part_splits[0], (TOKEN_COUNT, CONV_CH), 1.0, 6.0, ((0, 16),)),
        "conv_weight": normal_values(keys[1], (CONV, CONV_CH), CONV ** -0.5, 3.0, (), jnp.float32),
        "log_decay": draw_log_decay(jax.random.fold_in(jax.random.fold_in(keys[5], part), 71), part),
        "level_weight": jnp.clip(jnp.exp(math.log(2.0) - 1.3862944 * jax.random.uniform(part_splits[3], (LEVELS, HEADS, TOKEN_COUNT), jnp.float32) ** steps_of(part_splits[3], (LEVELS, HEADS, TOKEN_COUNT), ((2, 16),), -0.2, 0.2)), 0.5, 2.0),
        "grad_out": normal_values(part_splits[4], (TOKEN_COUNT, WIDTH), 0.25, 1.5, ((0, 16),)),
    }


def contract(formula, left_arg, right_arg):
    return jnp.einsum(formula, left_arg.astype(jnp.float32), right_arg.astype(jnp.float32), precision=lax.Precision.HIGHEST)

def by_head(state_arr, factor):
    head_count = factor.shape[-1]
    shaped = state_arr.reshape(state_arr.shape[:-1] + (head_count, state_arr.shape[-1] // head_count))
    return (shaped * factor[..., None, :, None]).reshape(state_arr.shape)

def per_token(values, factor):
    head_count = factor.shape[-1]
    shaped = values.reshape(values.shape[:-1] + (head_count, values.shape[-1] // head_count))
    return (shaped * factor[..., None]).reshape(values.shape)

def silu_slope(pre_act):
    sigmoid_val = jax.nn.sigmoid(pre_act)
    return sigmoid_val * (1.0 + pre_act * (1.0 - sigmoid_val))

def conv_apply(padded, weight, rows_dev):
    running_sum = jnp.zeros((rows_dev, weight.shape[1]), jnp.float32)
    for offset in range(weight.shape[0]):
        running_sum = running_sum + weight[offset] * padded[offset:offset + rows_dev].astype(jnp.float32)
    return running_sum

def conv_adjoint(padded_grad, weight, rows_dev):
    rim_rows = weight.shape[0] - 1
    running_sum = jnp.zeros((rows_dev, weight.shape[1]), jnp.float32)
    for offset in range(weight.shape[0]):
        running_sum = running_sum + weight[offset] * padded_grad[rim_rows - offset:rim_rows - offset + rows_dev]
    return running_sum

def conv_weight_grad(padded, grad_pre):
    rows_dev = grad_pre.shape[0]
    taps = padded.shape[0] - rows_dev + 1
    return jnp.stack([lax.optimization_barrier(jnp.sum(padded[offset:offset + rows_dev].astype(jnp.float32) * grad_pre, axis=0)) for offset in range(taps)])

def level_scale(level_idx, block_len):
    if level_idx == 0:
        return block_len ** (-0.5)
    return (block_len * 2 ** (level_idx - 1)) ** (-0.5)

def decay_tables(decay_rows, block_len):
    head_count, rows_dev = decay_rows.shape
    within = jnp.cumsum(decay_rows.reshape(head_count, rows_dev // block_len, block_len), axis=2)
    totals = within[:, :, -1]
    before = jnp.cumsum(totals, axis=1) - totals
    return (within, totals, before[:, :, None] + within, lax.optimization_barrier(jnp.sum(totals, axis=1)))

def span_levels(states, totals, near_count):
    head_count, blocks = totals.shape
    state_dim, channels = (states.shape[1], states.shape[2])
    before = jnp.cumsum(totals, axis=1) - totals
    block_ids = jnp.arange(blocks, dtype=jnp.int32)
    group_state = states
    group_total = totals
    starts = []
    for level_idx in range(near_count):
        half_id = block_ids >> level_idx
        upper = (half_id & 1).astype(jnp.float32)
        sibling = jnp.maximum(half_id - 1, 0).astype(jnp.int32)
        half_start = (half_id << level_idx).astype(jnp.int32)
        gap = before - before[:, half_start]
        factor = upper[None, :] * jnp.exp(gap)
        starts.append(by_head(group_state[sibling], factor.T))
        pairs = group_state.reshape(-1, 2, state_dim, channels)
        total_pairs = group_total.reshape(head_count, -1, 2)
        group_state = by_head(pairs[:, 0], jnp.exp(total_pairs[:, :, 1]).T) + pairs[:, 1]
        group_total = lax.optimization_barrier(jnp.sum(total_pairs, axis=2))
    return (jnp.stack(starts), group_state[0])

def far_inner(grad_rows, level_rows, scales, factor_rows, level_idx):
    return per_token(grad_rows, scales[level_idx] * level_rows[level_idx] * factor_rows)

def level_sums(grad_heads, output, scale_val):
    return scale_val * lax.optimization_barrier(jnp.sum(grad_heads * output.reshape(grad_heads.shape), axis=2)).T

def front_pass(u_act, decay_rows, level_weight, grad_out, far_count):
    rows_dev = u_act.shape[0]
    head_count = decay_rows.shape[0]
    channels = grad_out.shape[1]
    head_dim = channels // head_count
    state_dim = (u_act.shape[1] - channels) // 2
    block_len = BLOCK
    blocks = rows_dev // block_len
    near_count = blocks.bit_length() - 1
    far_base = 1 + near_count
    values_blk = u_act[:, :channels].reshape(blocks, block_len, head_count, head_dim)
    keys_blk = u_act[:, channels:channels + state_dim].reshape(blocks, block_len, state_dim)
    query_rows = u_act[:, channels + state_dim:]
    query_blk = query_rows.reshape(blocks, block_len, state_dim)
    within, totals, dev_cum, dev_total = decay_tables(decay_rows, block_len)
    in_block = jnp.exp(within).reshape(head_count, rows_dev).T
    in_device = jnp.exp(dev_cum).reshape(head_count, rows_dev).T
    level_rows = jnp.transpose(level_weight, (0, 2, 1))
    scales = [level_scale(level_idx, block_len) for level_idx in range(level_weight.shape[0])]
    grad_rows = grad_out.astype(jnp.float32)
    causal = jnp.arange(block_len)[:, None] >= jnp.arange(block_len)[None, :]
    score_gaps = jnp.where(causal, within[:, :, :, None] - within[:, :, None, :], 0.0)
    decay_mask = jnp.where(causal, jnp.exp(score_gaps), 0.0)
    scores = contract('kqn,ksn->kqs', query_blk, keys_blk)
    mixing = (scores[None] * decay_mask).astype(jnp.bfloat16)
    out_zero = contract('hkqs,kshp->kqhp', mixing, values_blk).reshape(rows_dev, channels)
    key_decay = jnp.exp(totals[:, :, None] - within)
    keys_scaled = (key_decay[..., None] * keys_blk[None].astype(jnp.float32)).astype(jnp.bfloat16)
    states = contract('hksn,kshp->knhp', keys_scaled, values_blk).reshape(blocks, state_dim, channels)

    def near_levels(block_arr):
        return span_levels(block_arr, totals, near_count)
    (starts_all, end_state), level_vjp = jax.vjp(near_levels, states)
    near_rows = contract('kqn,lknm->lkqm', query_blk, starts_all).reshape(near_count, rows_dev, channels)
    out_near = per_token(near_rows, jnp.broadcast_to(in_block, (near_count,) + in_block.shape))
    near_weight = jnp.stack([scales[1 + idx] * level_rows[1 + idx] for idx in range(near_count)])
    grad_zero = per_token(grad_rows, scales[0] * level_rows[0]).astype(jnp.bfloat16).reshape(blocks, block_len, head_count, head_dim)
    grad_mixing = contract('kqhp,kshp->hkqs', grad_zero, values_blk)
    grad_scores = lax.optimization_barrier(jnp.sum(grad_mixing * decay_mask, axis=0)).astype(jnp.bfloat16)
    grad_query = contract('kqs,ksn->kqn', grad_scores, keys_blk).reshape(rows_dev, state_dim)
    grad_key = contract('kqs,kqn->ksn', grad_scores, query_blk).reshape(rows_dev, state_dim)
    grad_value = contract('hkqs,kqhp->kshp', mixing, grad_zero).reshape(rows_dev, channels)
    grad_stack = jnp.broadcast_to(grad_rows, (near_count,) + grad_rows.shape)
    inner_near = per_token(grad_stack, near_weight * in_block[None]).reshape(near_count, blocks, block_len, channels)
    grad_query = grad_query + contract('lkqm,lknm->kqn', inner_near, starts_all).reshape(rows_dev, state_dim)
    grad_starts = contract('kqn,lkqm->lknm', query_blk, inner_near)
    grad_far = jnp.stack([contract('tn,tm->nm', query_rows, far_inner(grad_rows, level_rows, scales, in_device, far_base + level_idx)) for level_idx in range(far_count)])
    return dict(values_blk=values_blk, query_rows=query_rows, in_device=in_device, level_rows=level_rows, scales=scales, grad_rows=grad_rows, key_decay=key_decay, keys_scaled=keys_scaled, end_state=end_state, dev_total=dev_total, out_zero=out_zero, out_near=out_near, near_weight=near_weight, level_vjp=level_vjp, grad_query=grad_query, grad_key=grad_key, grad_value=grad_value, grad_starts=grad_starts, grad_far=grad_far)

def back_pass(pieces, far_states, grad_end, far_count):
    values_blk = pieces['values_blk']
    blocks, block_len, head_count, head_dim = values_blk.shape
    rows_dev = blocks * block_len
    channels = head_count * head_dim
    query_rows = pieces['query_rows']
    state_dim = query_rows.shape[1]
    level_rows = pieces['level_rows']
    scales = pieces['scales']
    grad_rows = pieces['grad_rows']
    in_device = pieces['in_device']
    out_near = pieces['out_near']
    near_count = out_near.shape[0]
    far_base = 1 + near_count
    grad_heads = grad_rows.reshape(rows_dev, head_count, head_dim)
    mixed_out = per_token(pieces['out_zero'], scales[0] * level_rows[0]) + lax.optimization_barrier(jnp.sum(per_token(out_near, pieces['near_weight']), axis=0))
    level_grads = [level_sums(grad_heads, pieces['out_zero'], scales[0])]
    for idx in range(near_count):
        level_grads.append(level_sums(grad_heads, out_near[idx], scales[1 + idx]))
    grad_query = pieces['grad_query']
    for level_idx in range(far_count):
        far_out = per_token(contract('tn,nm->tm', query_rows, far_states[level_idx]), in_device)
        mixed_out = mixed_out + per_token(far_out, scales[far_base + level_idx] * level_rows[far_base + level_idx])
        level_grads.append(level_sums(grad_heads, far_out, scales[far_base + level_idx]))
        inner_far = far_inner(grad_rows, level_rows, scales, in_device, far_base + level_idx)
        grad_query = grad_query + contract('tm,nm->tn', inner_far, far_states[level_idx])
    for level_idx in range(far_base + far_count, level_rows.shape[0]):
        level_grads.append(jnp.zeros((head_count, rows_dev), jnp.float32))
    grad_states = pieces['level_vjp']((pieces['grad_starts'], grad_end))[0]
    grad_four = grad_states.reshape(blocks, state_dim, head_count, head_dim)
    grad_scaled = contract('knhp,kshp->hksn', grad_four, values_blk)
    grad_key = pieces['grad_key'] + lax.optimization_barrier(jnp.sum(pieces['key_decay'][..., None] * grad_scaled, axis=0)).reshape(rows_dev, state_dim)
    grad_value = pieces['grad_value'] + contract('hksn,knhp->kshp', pieces['keys_scaled'], grad_four).reshape(rows_dev, channels)
    grad_act = jnp.concatenate([grad_value, grad_key, grad_query], axis=1)
    return (mixed_out, jnp.stack(level_grads), grad_act)

def fenwick_levels(end_states, device_decay, grad_fars, far_count):
    devices = end_states.shape[0]
    position = jnp.arange(devices, dtype=jnp.int32)
    running = end_states
    block_decay = device_decay
    prefix = jnp.ones_like(device_decay)
    far_states = []
    saved_steps = []
    for level_idx in range(far_count):
        partner = position ^ 1 << level_idx
        sib_state = running[partner]
        sib_decay = block_decay[partner]
        upper_half = (position >> level_idx & 1).astype(jnp.float32)[:, None]
        far_states.append(by_head(sib_state, upper_half * prefix))
        saved_steps.append((upper_half, prefix, block_decay, sib_decay, partner))
        running = by_head(sib_state, upper_half * block_decay + 1.0 - upper_half) + by_head(running, upper_half + (1.0 - upper_half) * sib_decay)
        prefix = prefix * (upper_half * sib_decay + 1.0 - upper_half)
        block_decay = block_decay * sib_decay
    back_grad = jnp.zeros_like(end_states)
    for level_idx in reversed(range(far_count)):
        upper_half, prefix, block_decay, sib_decay, partner = saved_steps[level_idx]
        outgoing = by_head(grad_fars[:, level_idx], upper_half * prefix) + by_head(back_grad, upper_half * block_decay + 1.0 - upper_half)
        back_grad = by_head(back_grad, upper_half + (1.0 - upper_half) * sib_decay) + outgoing[partner]
    return (jnp.stack(far_states, axis=1), back_grad)

def reference(conv_input, conv_weight, log_decay, level_weight, grad_out):
    devices = N_CTX
    rows_dev = TOK_DEV
    far_count = devices.bit_length() - 1
    rim_rows = conv_weight.shape[0] - 1
    conv_ch = conv_input.shape[1]
    head_count = log_decay.shape[0]
    level_count = level_weight.shape[0]
    input_blocks = conv_input.reshape(devices, rows_dev, conv_ch)
    prior_rows = jnp.concatenate([jnp.zeros((1, rim_rows, conv_ch), conv_input.dtype), input_blocks[:-1, rows_dev - rim_rows:]], axis=0)
    decay_blocks = log_decay.reshape(head_count, devices, rows_dev).transpose(1, 0, 2)
    weight_blocks = level_weight.reshape(level_count, head_count, devices, rows_dev).transpose(2, 0, 1, 3)
    grad_blocks = grad_out.reshape(devices, rows_dev, grad_out.shape[1])

    def activate(rows_in, rows_before):
        padded = jnp.concatenate([rows_before, rows_in], axis=0)
        pre_act = conv_apply(padded, conv_weight, rows_dev)
        return (padded, pre_act, jax.nn.silu(pre_act).astype(jnp.bfloat16))

    def first_pass(inputs):
        rows_in, rows_before, decay_rows, weight_rows, grad_rows = inputs
        padded, pre_act, u_act = activate(rows_in, rows_before)
        pieces = front_pass(u_act, decay_rows, weight_rows, grad_rows, far_count)
        return (pieces['end_state'], pieces['dev_total'], pieces['grad_far'])
    end_states, dev_totals, grad_fars = lax.map(first_pass, (input_blocks, prior_rows, decay_blocks, weight_blocks, grad_blocks))
    far_all, grad_ends = fenwick_levels(end_states, jnp.exp(dev_totals), grad_fars, far_count)

    def second_pass(inputs):
        rows_in, rows_before, decay_rows, weight_rows, grad_rows, far_rows, grad_end = inputs
        padded, pre_act, u_act = activate(rows_in, rows_before)
        pieces = front_pass(u_act, decay_rows, weight_rows, grad_rows, far_count)
        mixed_out, level_grad, grad_act = back_pass(pieces, far_rows, grad_end, far_count)
        grad_pre = grad_act * silu_slope(pre_act)
        weight_part = conv_weight_grad(padded, grad_pre)
        padded_grad = jnp.concatenate([grad_pre, jnp.zeros((rim_rows, conv_ch), jnp.float32)], axis=0)
        local_in = conv_adjoint(padded_grad, conv_weight, rows_dev)
        return (mixed_out.astype(jnp.bfloat16), level_grad, grad_pre[:rim_rows], local_in[:rows_dev - rim_rows].astype(jnp.bfloat16), local_in[rows_dev - rim_rows:], weight_part)
    mixed_blocks, level_blocks, head_rows, main_rows, tail_rows, weight_parts = lax.map(second_pass, (input_blocks, prior_rows, decay_blocks, weight_blocks, grad_blocks, far_all, grad_ends))
    next_heads = jnp.concatenate([head_rows[1:], jnp.zeros((1, rim_rows, conv_ch), jnp.float32)], axis=0)

    def tail_terms(rows_after):
        return conv_adjoint(jnp.concatenate([jnp.zeros((rim_rows, conv_ch), jnp.float32), rows_after], axis=0), conv_weight, rim_rows)
    tails = (tail_rows + jax.vmap(tail_terms)(next_heads)).astype(jnp.bfloat16)
    grad_input = jnp.concatenate([main_rows, tails], axis=1).reshape(devices * rows_dev, conv_ch)
    mixed = mixed_blocks.reshape(devices * rows_dev, mixed_blocks.shape[2])
    grad_level = level_blocks.transpose(1, 2, 0, 3).reshape(level_count, head_count, devices * rows_dev)
    grad_conv = lax.optimization_barrier(jnp.sum(weight_parts, axis=0))
    return (mixed, grad_input, grad_level, grad_conv)
```

```python
import functools

import jax
import jax.numpy as jnp
from jax import lax
from jax.experimental import pallas as pl
from jax.experimental.pallas import tpu as pltpu
from jax.sharding import PartitionSpec as P

BLOCK = 64
LANES = 128
MESH = pl.DeviceIdType.MESH
HIGH = lax.Precision.HIGHEST
F32 = jnp.float32
BF16 = jnp.bfloat16
VMEM_LIMIT = 56 * 1024 * 1024


def level_scale(level_idx):
    if level_idx == 0:
        return BLOCK**-0.5
    return (BLOCK * 2 ** (level_idx - 1)) ** -0.5


def dot(a, b):
    return jnp.dot(a, b, preferred_element_type=F32)


def dot_nt(a, b):
    return lax.dot_general(a, b, (((1,), (1,)), ((), ())), preferred_element_type=F32)


def split2(v):
    hi = v.astype(BF16)
    return hi, (v - hi.astype(F32)).astype(BF16)


def split3(v):
    hi = v.astype(BF16)
    rest = v - hi.astype(F32)
    mid = rest.astype(BF16)
    return hi, mid, (rest - mid.astype(F32)).astype(BF16)


def iota(shape, axis):
    return lax.broadcasted_iota(jnp.int32, shape, axis)


def one_hot(rows, heads, first, lanes, width):
    return jnp.where(
        iota((rows, lanes), 0) % heads == first + iota((rows, lanes), 1) // width, 1.0, 0.0
    ).astype(BF16)


def greet(peers):
    barrier = pltpu.get_barrier_semaphore()
    for peer in peers:
        pl.semaphore_signal(barrier, inc=1, device_id=peer, device_id_type=MESH)
    pl.semaphore_wait(barrier, len(peers))


def at(peer):
    return (lax.axis_index("groups"), peer)


def edge_kernel(n, conv_ref, decay_ref, prior_ref, totals_ref, mine, slots, rows, send, recv, rsend, rrecv):
    me = lax.axis_index("ctx")
    peers = [lax.rem(me + d, n) for d in range(1, n)]
    heads = decay_ref.shape[0]
    mine[...] = jnp.zeros_like(mine)
    mine[:, :heads] = lax.dot_general(
        jnp.ones((8, decay_ref.shape[1]), F32),
        decay_ref[...],
        (((1,), (1,)), ((), ())),
        precision=HIGH,
        preferred_element_type=F32,
    )
    greet([at(p) for p in peers])
    copies = []
    count = conv_ref.shape[0]
    row_copy = pltpu.make_async_remote_copy(
        conv_ref.at[pl.ds(count - 16, 16), :], rows, rsend, rrecv, at(peers[0]), MESH
    )
    row_copy.start()
    for d in range(1, n):
        copy = pltpu.make_async_remote_copy(
            mine, slots.at[d - 1], send.at[d - 1], recv.at[d - 1], at(peers[d - 1]), MESH
        )
        copy.start()
        copies.append(copy)
    totals_ref[me] = mine[...]
    for d in range(1, n):
        copies[d - 1].wait()
        totals_ref[lax.rem(me - d + n, n)] = slots[d - 1]
    row_copy.wait()
    keep = jnp.where(me > 0, 1.0, 0.0)
    prior_ref[...] = (rows[...].astype(F32) * keep).astype(BF16)


def exchange_edges(n, conv_input, log_decay):
    channels = conv_input.shape[1]
    vm = pl.BlockSpec(memory_space=pltpu.VMEM)
    return pl.pallas_call(
        functools.partial(edge_kernel, n),
        out_shape=(
            jax.ShapeDtypeStruct((16, channels), BF16),
            jax.ShapeDtypeStruct((n, 8, LANES), F32),
        ),
        in_specs=[vm, vm],
        out_specs=(vm, vm),
        scratch_shapes=[
            pltpu.VMEM((8, LANES), F32),
            pltpu.VMEM((n - 1, 8, LANES), F32),
            pltpu.VMEM((16, channels), BF16),
            pltpu.SemaphoreType.DMA((n - 1,)),
            pltpu.SemaphoreType.DMA((n - 1,)),
            pltpu.SemaphoreType.DMA,
            pltpu.SemaphoreType.DMA,
        ],
        compiler_params=pltpu.CompilerParams(
            collective_id=0, has_side_effects=True, vmem_limit_bytes=VMEM_LIMIT
        ),
    )(conv_input, log_decay)


def fill_padded(pad, conv_ref, prior_ref):
    pad[0:8, :] = prior_ref[...].astype(F32)[8:16]
    pad[8:, :] = conv_ref[...].astype(F32)


def running_decay(decay_ref):
    rows = decay_ref.shape[1]
    lower = jnp.where(iota((rows, rows), 0) >= iota((rows, rows), 1), 1.0, 0.0)
    by_token = jnp.dot(lower, decay_ref[...].T, precision=HIGH, preferred_element_type=F32)
    return by_token


def front_kernel(
    far, conv_ref, prior_ref, w_ref, decay_ref, lw_ref, g_ref, totals_ref,
    u_ref, slope_ref, end_ref, gf_ref, fac_ref, pad, facs,
):
    me = lax.axis_index("ctx")
    rows, channels = g_ref.shape
    heads = decay_ref.shape[0]
    taps = w_ref.shape[0]
    fill_padded(pad, conv_ref, prior_ref)
    totals = totals_ref[...][:, 0, :heads]
    spans = iota(totals.shape, 0)

    def span(lo, hi):
        return jnp.sum(jnp.where((spans >= lo) & (spans < hi), totals, 0.0), axis=0, keepdims=True)

    own, pre = [], []
    for level in range(far):
        half = me >> level
        upper = (half & 1) == 1
        start = half << level
        sib = (half ^ 1) << level
        size = 1 << level
        own.append(jnp.exp(jnp.where(upper, 0.0, 1.0) * span(sib, sib + size)))
        own.append(jnp.exp(jnp.where(upper, 1.0, 0.0) * span(start, start + size)))
        pre.append(jnp.where(upper, 1.0, 0.0) * jnp.exp(span(start, me)))
    count = fac_ref.shape[1]
    stack = own + pre
    if count > len(stack):
        stack.append(jnp.zeros((count - len(stack), heads), F32))
    small = jnp.concatenate(split2(jnp.concatenate(stack, axis=0)), axis=1)

    cum = running_decay(decay_ref)
    in_device = jnp.exp(cum)
    base = [jnp.exp(cum[rows - 1 : rows] - cum)]
    for level in range(far):
        base.append(in_device * lw_ref[2 + level].T * (level_scale(2 + level) * pre[level]))
    for idx, value in enumerate(base):
        facs[idx * rows : (idx + 1) * rows, :] = jnp.concatenate(split2(value), axis=1)

    def activate(cols):
        acc = w_ref[0:1, cols] * pad[8 - taps + 1 : 8 - taps + 1 + rows, cols]
        for k in range(1, taps):
            acc = acc + w_ref[k : k + 1, cols] * pad[8 - taps + 1 + k : 8 - taps + 1 + k + rows, cols]
        sig = jax.nn.sigmoid(acc)
        u = (acc * sig).astype(BF16)
        u_ref[:, cols] = u
        slope_ref[:, cols] = sig * (1.0 + acc * (1.0 - sig))
        return u

    bq = activate(pl.ds(channels, LANES)).astype(F32).T.astype(BF16)
    b_t = jnp.concatenate([bq[:BLOCK]] * 2, axis=1)
    q_t = jnp.concatenate([bq[BLOCK:]] * 2, axis=1)
    per_half = channels // 2 // LANES

    @pl.loop(0, channels // LANES)
    def _(j):
        cols = pl.ds(pl.multiple_of(j * LANES, LANES), LANES)
        side = j // per_half
        out = pl.ds(pl.multiple_of((j % per_half) * LANES, LANES), LANES)
        x = activate(cols).astype(F32)
        hot = one_hot(2 * heads, heads, 2 * j, LANES, BLOCK)
        spread = dot(facs[...], hot)
        fac_ref[side, :, out] = dot(small, hot)
        end_ref[side, :, out] = dot(b_t, jnp.concatenate(split2(x * spread[:rows]), axis=0))
        g = g_ref[:, cols].astype(F32)
        for level in range(far):
            inner = g * spread[(1 + level) * rows : (2 + level) * rows]
            gf_ref[level, side, :, out] = dot(q_t, jnp.concatenate(split2(inner), axis=0))


def fenwick_kernel(
    far, end_ref, gf_ref, fac_ref, far_ref, grad_ref,
    up0, up0_in, up, up_in, cross_in, merge, merge_in, down, down_in, last, last_in,
    sems_s, sems_r, run, back,
):
    me = lax.axis_index("ctx")
    core = me & 1
    other = 1 - core
    peers = [at(me ^ (1 << level)) for level in range(far)]

    def copy(src, dst, kind, level, peer):
        made = pltpu.make_async_remote_copy(
            src, dst, sems_s.at[kind, level], sems_r.at[kind, level], peer, MESH
        )
        made.start()
        return made

    pending = []
    up0[...] = end_ref[...].astype(BF16)
    for level in range(1, far):
        merge[level - 1] = gf_ref[level, other].astype(BF16)
    greet(peers)
    merge_copy = copy(merge, merge_in, 0, 0, peers[0])
    up_copy = copy(up0, up0_in, 1, 0, peers[0])
    crosses = []

    def own_coef(level):
        return fac_ref[core, 2 * level : 2 * level + 1, :]

    def sib_coef(level):
        return fac_ref[core, 2 * level + 1 : 2 * level + 2, :]

    merge_copy.wait()
    pending_down = None
    for step in range(far - 1):
        level = far - 1 - step
        total = gf_ref[level, core] + merge_in[level - 1].astype(F32)
        if step > 0:
            pending_down.wait()
            back[...] = back[...] * own_coef(level + 1) if step > 1 else jnp.zeros_like(back)
            back[...] = back[...] + down_in[level].astype(F32)
            total = total + back[...] * sib_coef(level)
        down[level - 1] = total.astype(BF16)
        pending_down = copy(down.at[level - 1], down_in.at[level - 1], 2, level, peers[level])

        up_copy.wait()
        if step == 0:
            run[...] = end_ref[core] * own_coef(0) + up0_in[core].astype(F32) * sib_coef(0)
        else:
            crosses.append(copy(up_in.at[step - 1], cross_in.at[step - 1], 3, step, peers[0]))
            run[...] = run[...] * own_coef(step) + up_in[step - 1].astype(F32) * sib_coef(step)
        up[step] = run[...].astype(BF16)
        up_copy = copy(up.at[step], up_in.at[step], 1, step + 1, peers[step + 1])
    pending_down.wait()
    if far > 2:
        back[...] = back[...] * own_coef(1) + down_in[0].astype(F32)
    else:
        back[...] = down_in[0].astype(F32)
    last[core] = (gf_ref[0, core] + back[...] * sib_coef(0)).astype(BF16)
    last[other] = gf_ref[0, other].astype(BF16)
    last_copy = copy(last, last_in, 4, 0, peers[0])
    up_copy.wait()
    crosses.append(copy(up_in.at[far - 2], cross_in.at[far - 2], 3, far - 1, peers[0]))
    far_ref[0] = up0_in[...]
    for level in range(1, far):
        far_ref[level, core] = up_in[level - 1]
    last_copy.wait()
    grad_ref[core] = back[...] * own_coef(0) + last_in[core].astype(F32)
    grad_ref[other] = last_in[other].astype(F32)
    for level in range(1, far):
        crosses[level - 1].wait()
        far_ref[level, other] = cross_in[level - 1]


def exchange_states(far, end_state, grad_far, factors):
    half = end_state.shape
    piece = half[1:]
    vm = pl.BlockSpec(memory_space=pltpu.VMEM)
    stack = (far - 1,) + piece
    return pl.pallas_call(
        functools.partial(fenwick_kernel, far),
        out_shape=(
            jax.ShapeDtypeStruct((far,) + half, BF16),
            jax.ShapeDtypeStruct(half, F32),
        ),
        in_specs=[vm] * 3,
        out_specs=(vm, vm),
        scratch_shapes=[
            pltpu.VMEM(half, BF16),
            pltpu.VMEM(half, BF16),
            pltpu.VMEM(stack, BF16),
            pltpu.VMEM(stack, BF16),
            pltpu.VMEM(stack, BF16),
            pltpu.VMEM(stack, BF16),
            pltpu.VMEM(stack, BF16),
            pltpu.VMEM(stack, BF16),
            pltpu.VMEM(stack, BF16),
            pltpu.VMEM(half, BF16),
            pltpu.VMEM(half, BF16),
            pltpu.SemaphoreType.DMA((5, far)),
            pltpu.SemaphoreType.DMA((5, far)),
            pltpu.VMEM(piece, F32),
            pltpu.VMEM(piece, F32),
        ],
        compiler_params=pltpu.CompilerParams(
            collective_id=1, has_side_effects=True, vmem_limit_bytes=VMEM_LIMIT
        ),
    )(end_state, grad_far, factors)


def back_kernel(
    far, conv_ref, prior_ref, w_ref, decay_ref, lw_ref, g_ref, u_ref, slope_ref, fac_ref, far_ref, grad_ref,
    mixed_ref, gin_ref, glev_ref, tail_ref, head_ref, wpart_ref,
    pad, gp, facs, cum3, cum_rows, bias, scores, hotx, hotg, q_s, b2_s, ds_acc, dq_acc, db_acc,
):
    rows, channels = g_ref.shape
    heads = decay_ref.shape[0]
    taps = w_ref.shape[0]
    wide = 2 * rows
    fill_padded(pad, conv_ref, prior_ref)
    cum = running_decay(decay_ref)
    cum_rows[...] = cum.T
    cum3[...] = jnp.concatenate(split3(cum), axis=1)
    base = [lw_ref[0].T * level_scale(0), lw_ref[1].T * level_scale(1)]
    base += [jnp.exp(cum[rows - 1 : rows] - cum), jnp.exp(cum)]
    base += [lw_ref[2 + level].T * level_scale(2 + level) for level in range(far)]
    for idx, value in enumerate(base):
        facs[idx * rows : (idx + 1) * rows, :] = jnp.concatenate(split2(value), axis=1)
    first = iota((rows, wide), 0)
    second = iota((rows, wide), 1) % rows
    bias[0] = jnp.where(second <= first, 0.0, -1e30)
    bias[1] = jnp.where(first <= second, 0.0, -1e30)
    r, c = iota((wide, wide), 0), iota((wide, wide), 1)
    same = (r // rows) == (c % LANES) // BLOCK
    block1 = (r % rows) // BLOCK == 1
    hotg[...] = jnp.where(same, 1.0, 0.0).astype(BF16)
    hotx[...] = jnp.where(same & (block1 == (c < LANES)), 1.0, 0.0).astype(BF16)
    bq = u_ref[:, channels:]
    b, q = bq[:, :BLOCK], bq[:, BLOCK:]
    q_s[...] = q
    b2_s[...] = jnp.concatenate([b, b], axis=1)
    scores[0] = dot_nt(q, jnp.concatenate([b, b], axis=0))
    scores[1] = dot_nt(b, jnp.concatenate([q, q], axis=0))
    ds_acc[...] = jnp.zeros_like(ds_acc)
    dq_acc[...] = jnp.zeros_like(dq_acc)
    db_acc[...] = jnp.zeros_like(db_acc)
    glev_ref[...] = jnp.zeros_like(glev_ref)
    per_half = channels // 2 // LANES
    low = iota((rows, LANES), 0) < BLOCK

    @pl.loop(0, channels // LANES)
    def _(j):
        cols = pl.ds(pl.multiple_of(j * LANES, LANES), LANES)
        side = j // per_half
        part = pl.ds(pl.multiple_of((j % per_half) * LANES, LANES), LANES)
        x = u_ref[:, cols]
        g = g_ref[:, cols].astype(F32)
        spread = dot(facs[...], one_hot(2 * heads, heads, 2 * j, LANES, BLOCK))

        def fac(idx):
            return spread[idx * rows : (idx + 1) * rows]

        w0, w1 = fac(0), fac(1)
        col = dot(cum3[...], one_hot(3 * heads, heads, 2 * j, wide, rows))
        row = jnp.concatenate([cum_rows[pl.ds(2 * j, 1), :], cum_rows[pl.ds(2 * j + 1, 1), :]], axis=1)
        gap = col - row
        decay = jnp.exp(gap + bias[0])
        mix = (scores[0] * decay).astype(BF16)
        mix_t = (scores[1] * jnp.exp(bias[1] - gap)).astype(BF16)
        wx = jnp.concatenate([jnp.concatenate([x, x], axis=1)] * 2, axis=0) * hotx[...]
        res = dot(mix, wx)
        out0 = jnp.where(low, res[:, LANES:], res[:, :LANES])
        out1 = jnp.where(low, 0.0, res[:, LANES:])
        gz = (g * w0).astype(BF16)
        gh = (g * jnp.where(low, w0, w1)).astype(BF16)
        gg = jnp.concatenate([gz, gh], axis=1)
        ds_acc[...] += decay * dot_nt(gg, wx)
        res = dot(mix_t, jnp.concatenate([gg, gg], axis=0) * hotg[...])
        dx = jnp.where(low, res[:, LANES:], res[:, :LANES])

        mixed = w0 * out0 + w1 * out1
        products = [g * out0, g * out1]
        inner, states = [], []
        for level in range(far):
            state = far_ref[level, side, :, part]
            scale = fac(3) * fac_ref[side, 2 * far + level : 2 * far + level + 1, part]
            out = dot(q_s[...], state) * scale
            weight = fac(4 + level)
            mixed = mixed + weight * out
            products.append(g * out)
            inner.append((g * weight * scale).astype(BF16))
            states.append(state)
        mixed_ref[:, cols] = mixed.astype(BF16)
        dq_acc[...] += dot_nt(jnp.concatenate(inner, axis=1), jnp.concatenate(states, axis=1))
        pick = jnp.where(
            iota((heads, 2 * LANES), 0) == 2 * j + (iota((heads, 2 * LANES), 1) % LANES) // BLOCK, 1.0, 0.0
        ).astype(BF16)
        for level, product in enumerate(products):
            glev_ref[level] += dot_nt(pick, jnp.concatenate(split2(product), axis=1)) * level_scale(level)

        grad = grad_ref[side, :, part]
        hi, lo = split2(grad)
        key_decay = fac(2)
        dx = dx + key_decay * dot(b2_s[...], jnp.concatenate([hi, lo], axis=0))
        db_acc[...] += dot_nt((x.astype(F32) * key_decay).astype(BF16), hi)
        gp[0:rows, cols] = dx * slope_ref[:, cols]

    ds = ds_acc[:, :rows] + ds_acc[:, rows:]
    dq = dq_acc[...] + dot(ds.astype(BF16), b)
    db = db_acc[...] + dot(ds.T.astype(BF16), q)
    gp[0:rows, channels:] = jnp.concatenate([db, dq], axis=1) * slope_ref[:, channels:]
    gp[rows:, :] = jnp.zeros((8, gp.shape[1]), F32)
    head_ref[...] = gp[0:8, :]

    @pl.loop(0, gp.shape[1] // LANES)
    def _(j):
        cols = pl.ds(pl.multiple_of(j * LANES, LANES), LANES)
        grad = gp[0:rows, cols]
        acc = w_ref[taps - 1 : taps, cols] * grad
        sums = []
        for k in range(taps):
            shift = taps - 1 - k
            if shift:
                acc = acc + w_ref[k : k + 1, cols] * gp[shift : shift + rows, cols]
            sums.append(jnp.sum(pad[8 - shift : 8 - shift + rows, cols] * grad, axis=0, keepdims=True))
        gin_ref[:, cols] = acc.astype(BF16)
        tail_ref[:, cols] = acc[rows - 16 :]
        sums.append(jnp.zeros((8 - taps, LANES), F32))
        wpart_ref[:, cols] = jnp.concatenate(sums, axis=0)


def finish_kernel(n, digits, tail_ref, head_ref, wpart_ref, w_ref, out_ref, wsum_ref, nxt, acc, slots, hs, hr, send, recv):
    me = lax.axis_index("ctx")
    taps = w_ref.shape[0]
    before, after = lax.rem(me + n - 1, n), lax.rem(me + 1, n)
    plan = []
    for shift, size in digits:
        digit = (me >> shift) & (size - 1)
        plan.append((digit, [me ^ (d << shift) for d in range(1, size)]))
    greet([at(before), at(after)] + [at(p) for _, peers in plan for p in peers])
    row_copy = pltpu.make_async_remote_copy(head_ref, nxt, hs, hr, at(before), MESH)
    row_copy.start()
    acc[0] = wpart_ref[...]
    for stage, (digit, peers) in enumerate(plan):
        copies = []
        for d, peer in enumerate(peers):
            copy = pltpu.make_async_remote_copy(
                acc.at[stage], slots.at[stage, d], send.at[stage, d], recv.at[stage, d], at(peer), MESH
            )
            copy.start()
            copies.append(copy)
        if stage == 0:
            row_copy.wait()
            keep = jnp.where(me < n - 1, 1.0, 0.0)
            rows = nxt[...] * keep
            joined = jnp.concatenate([jnp.zeros((8, rows.shape[1]), F32), rows], axis=0)
            fix = jnp.zeros((8, rows.shape[1]), F32)
            for k in range(taps - 1):
                shift = taps - 1 - k
                fix = fix + w_ref[k : k + 1, :] * joined[shift : shift + 8]
            out_ref[...] = (tail_ref[...] + jnp.concatenate([jnp.zeros_like(fix), fix], axis=0)).astype(BF16)
        for copy in copies:
            copy.wait()
        size = len(peers) + 1
        have = [acc[stage]] + [slots[stage, d] for d in range(size - 1)]
        if size == 2:
            total = have[0] + have[1]
        else:
            total = (have[0] + have[1]) + (have[2] + have[3])
        acc[stage + 1] = total
    wsum_ref[...] = acc[len(plan)][:taps]


def exchange_finish(n, tail, head, wpart, conv_weight):
    far = n.bit_length() - 1
    digits = []
    shift = 0
    while shift < far:
        bits = min(2, far - shift)
        digits.append((shift, 1 << bits))
        shift += bits
    channels = tail.shape[1]
    vm = pl.BlockSpec(memory_space=pltpu.VMEM)
    return pl.pallas_call(
        functools.partial(finish_kernel, n, digits),
        out_shape=(
            jax.ShapeDtypeStruct((16, channels), BF16),
            jax.ShapeDtypeStruct(conv_weight.shape, F32),
        ),
        in_specs=[vm] * 4,
        out_specs=(vm, vm),
        scratch_shapes=[
            pltpu.VMEM((8, channels), F32),
            pltpu.VMEM((len(digits) + 1, 8, channels), F32),
            pltpu.VMEM((len(digits), 3, 8, channels), F32),
            pltpu.SemaphoreType.DMA,
            pltpu.SemaphoreType.DMA,
            pltpu.SemaphoreType.DMA((len(digits), 3)),
            pltpu.SemaphoreType.DMA((len(digits), 3)),
        ],
        compiler_params=pltpu.CompilerParams(
            collective_id=2, has_side_effects=True, vmem_limit_bytes=VMEM_LIMIT
        ),
    )(tail, head, wpart, conv_weight)


def body(conv_input, conv_weight, log_decay, level_weight, grad_out):
    n = lax.axis_size("ctx")
    far = n.bit_length() - 1
    rows, conv_ch = conv_input.shape
    channels = grad_out.shape[1]
    heads = log_decay.shape[0]
    vm = pl.BlockSpec(memory_space=pltpu.VMEM)
    params = pltpu.CompilerParams(vmem_limit_bytes=VMEM_LIMIT)
    shape = jax.ShapeDtypeStruct
    half = (2, BLOCK, channels // 2)
    fac_rows = (3 * far + 7) // 8 * 8
    prior, totals = exchange_edges(n, conv_input, log_decay)
    u_act, slope, end_state, grad_far, factors = pl.pallas_call(
        functools.partial(front_kernel, far),
        out_shape=(
            shape((rows, conv_ch), BF16),
            shape((rows, conv_ch), F32),
            shape(half, F32),
            shape((far,) + half, F32),
            shape((2, fac_rows, channels // 2), F32),
        ),
        in_specs=[vm] * 7,
        out_specs=(vm,) * 5,
        scratch_shapes=[
            pltpu.VMEM((rows + 8, conv_ch), F32),
            pltpu.VMEM(((1 + far) * rows, 2 * heads), BF16),
        ],
        compiler_params=params,
    )(conv_input, prior, conv_weight, log_decay, level_weight, grad_out, totals)
    far_states, grad_end = exchange_states(far, end_state, grad_far, factors)
    mixed, grad_input, grad_level, tail, head, wpart = pl.pallas_call(
        functools.partial(back_kernel, far),
        out_shape=(
            shape((rows, channels), BF16),
            shape((rows, conv_ch), BF16),
            shape(level_weight.shape, F32),
            shape((16, conv_ch), F32),
            shape((8, conv_ch), F32),
            shape((8, conv_ch), F32),
        ),
        in_specs=[vm] * 11,
        out_specs=(vm,) * 6,
        scratch_shapes=[
            pltpu.VMEM((rows + 8, conv_ch), F32),
            pltpu.VMEM((rows + 8, conv_ch), F32),
            pltpu.VMEM(((4 + far) * rows, 2 * heads), BF16),
            pltpu.VMEM((rows, 3 * heads), BF16),
            pltpu.VMEM((heads, rows), F32),
            pltpu.VMEM((2, rows, 2 * rows), F32),
            pltpu.VMEM((2, rows, 2 * rows), F32),
            pltpu.VMEM((2 * rows, 2 * rows), BF16),
            pltpu.VMEM((2 * rows, 2 * rows), BF16),
            pltpu.VMEM((rows, BLOCK), BF16),
            pltpu.VMEM((rows, 2 * BLOCK), BF16),
            pltpu.VMEM((rows, 2 * rows), F32),
            pltpu.VMEM((rows, BLOCK), F32),
            pltpu.VMEM((rows, BLOCK), F32),
        ],
        compiler_params=params,
    )(
        conv_input, prior, conv_weight, log_decay, level_weight, grad_out,
        u_act, slope, factors, far_states, grad_end,
    )
    tail_rows, weight_grad = exchange_finish(n, tail, head, wpart, conv_weight)
    grad_input = lax.dynamic_update_slice(grad_input, tail_rows, (rows - 16, 0))
    return (mixed, grad_input, grad_level, weight_grad)


def solution(mesh):
    in_specs = (
        P(("groups", "ctx"), None),
        P(),
        P(None, ("groups", "ctx")),
        P(None, None, ("groups", "ctx")),
        P(("groups", "ctx"), None),
    )
    out_specs = (
        P(("groups", "ctx"), None),
        P(("groups", "ctx"), None),
        P(None, None, ("groups", "ctx")),
        P("groups", None),
    )
    return jax.shard_map(body, mesh=mesh, in_specs=in_specs, out_specs=out_specs, check_vma=False)
```

```python
import functools

import jax
import jax.numpy as jnp
from jax import lax
from jax.experimental import pallas as pl
from jax.experimental.pallas import tpu as pltpu
from jax.sharding import PartitionSpec as P

BLOCK = 64
LANES = 128
MESH = pl.DeviceIdType.MESH
HIGH = lax.Precision.HIGHEST
F32 = jnp.float32
BF16 = jnp.bfloat16
VMEM_LIMIT = 56 * 1024 * 1024


def level_scale(level_idx):
    if level_idx == 0:
        return BLOCK**-0.5
    return (BLOCK * 2 ** (level_idx - 1)) ** -0.5


def dot(a, b):
    return jnp.dot(a, b, preferred_element_type=F32)


def dot_nt(a, b):
    return lax.dot_general(a, b, (((1,), (1,)), ((), ())), preferred_element_type=F32)


def split2(v):
    hi = v.astype(BF16)
    return hi, (v - hi.astype(F32)).astype(BF16)


def split3(v):
    hi = v.astype(BF16)
    rest = v - hi.astype(F32)
    mid = rest.astype(BF16)
    return hi, mid, (rest - mid.astype(F32)).astype(BF16)


def iota(shape, axis):
    return lax.broadcasted_iota(jnp.int32, shape, axis)


def one_hot(rows, heads, first, lanes, width):
    return jnp.where(
        iota((rows, lanes), 0) % heads == first + iota((rows, lanes), 1) // width, 1.0, 0.0
    ).astype(BF16)


def greet(peers):
    barrier = pltpu.get_barrier_semaphore()
    for peer in peers:
        pl.semaphore_signal(barrier, inc=1, device_id=peer, device_id_type=MESH)
    pl.semaphore_wait(barrier, len(peers))


def at(peer):
    return (lax.axis_index("groups"), peer)


def edge_kernel(n, conv_ref, decay_ref, prior_ref, totals_ref, mine, slots, rows, send, recv, rsend, rrecv):
    me = lax.axis_index("ctx")
    peers = [lax.rem(me + d, n) for d in range(1, n)]
    heads = decay_ref.shape[0]
    mine[...] = jnp.zeros_like(mine)
    mine[:, :heads] = lax.dot_general(
        jnp.ones((8, decay_ref.shape[1]), F32),
        decay_ref[...],
        (((1,), (1,)), ((), ())),
        precision=HIGH,
        preferred_element_type=F32,
    )
    greet([at(p) for p in peers])
    copies = []
    count = conv_ref.shape[0]
    row_copy = pltpu.make_async_remote_copy(
        conv_ref.at[pl.ds(count - 16, 16), :], rows, rsend, rrecv, at(peers[0]), MESH
    )
    row_copy.start()
    for d in range(1, n):
        copy = pltpu.make_async_remote_copy(
            mine, slots.at[d - 1], send.at[d - 1], recv.at[d - 1], at(peers[d - 1]), MESH
        )
        copy.start()
        copies.append(copy)
    totals_ref[me] = mine[...]
    for d in range(1, n):
        copies[d - 1].wait()
        totals_ref[lax.rem(me - d + n, n)] = slots[d - 1]
    row_copy.wait()
    keep = jnp.where(me > 0, 1.0, 0.0)
    prior_ref[...] = (rows[...].astype(F32) * keep).astype(BF16)


def exchange_edges(n, conv_input, log_decay):
    channels = conv_input.shape[1]
    vm = pl.BlockSpec(memory_space=pltpu.VMEM)
    return pl.pallas_call(
        functools.partial(edge_kernel, n),
        out_shape=(
            jax.ShapeDtypeStruct((16, channels), BF16),
            jax.ShapeDtypeStruct((n, 8, LANES), F32),
        ),
        in_specs=[pl.BlockSpec(memory_space=pl.ANY), vm],
        out_specs=(vm, vm),
        scratch_shapes=[
            pltpu.VMEM((8, LANES), F32),
            pltpu.VMEM((n - 1, 8, LANES), F32),
            pltpu.VMEM((16, channels), BF16),
            pltpu.SemaphoreType.DMA((n - 1,)),
            pltpu.SemaphoreType.DMA((n - 1,)),
            pltpu.SemaphoreType.DMA,
            pltpu.SemaphoreType.DMA,
        ],
        compiler_params=pltpu.CompilerParams(
            collective_id=0, has_side_effects=True, vmem_limit_bytes=VMEM_LIMIT
        ),
    )(conv_input, log_decay)


def fill_padded(pad, conv_ref, prior_ref):
    pad[0:8, :] = prior_ref[...].astype(F32)[8:16]
    pad[8:, :] = conv_ref[...].astype(F32)


def running_decay(decay_ref):
    rows = decay_ref.shape[1]
    lower = jnp.where(iota((rows, rows), 0) >= iota((rows, rows), 1), 1.0, 0.0)
    by_token = jnp.dot(lower, decay_ref[...].T, precision=HIGH, preferred_element_type=F32)
    return by_token


def front_kernel(
    far, conv_ref, prior_ref, w_ref, decay_ref, lw_ref, g_ref, totals_ref,
    u_ref, slope_ref, end_ref, gf_ref, fac_ref, pad, facs,
):
    me = lax.axis_index("ctx")
    rows, channels = g_ref.shape
    heads = decay_ref.shape[0]
    taps = w_ref.shape[0]
    fill_padded(pad, conv_ref, prior_ref)
    totals = totals_ref[...][:, 0, :heads]
    spans = iota(totals.shape, 0)

    def span(lo, hi):
        return jnp.sum(jnp.where((spans >= lo) & (spans < hi), totals, 0.0), axis=0, keepdims=True)

    own, pre = [], []
    for level in range(far):
        half = me >> level
        upper = (half & 1) == 1
        start = half << level
        sib = (half ^ 1) << level
        size = 1 << level
        own.append(jnp.exp(jnp.where(upper, 0.0, 1.0) * span(sib, sib + size)))
        own.append(jnp.exp(jnp.where(upper, 1.0, 0.0) * span(start, start + size)))
        pre.append(jnp.where(upper, 1.0, 0.0) * jnp.exp(span(start, me)))
    count = fac_ref.shape[1]
    stack = own + pre
    if count > len(stack):
        stack.append(jnp.zeros((count - len(stack), heads), F32))
    small = jnp.concatenate(split2(jnp.concatenate(stack, axis=0)), axis=1)

    cum = running_decay(decay_ref)
    in_device = jnp.exp(cum)
    base = [jnp.exp(cum[rows - 1 : rows] - cum)]
    for level in range(far):
        base.append(in_device * lw_ref[2 + level].T * (level_scale(2 + level) * pre[level]))
    for idx, value in enumerate(base):
        facs[idx * rows : (idx + 1) * rows, :] = jnp.concatenate(split2(value), axis=1)

    def activate(cols):
        acc = w_ref[0:1, cols] * pad[8 - taps + 1 : 8 - taps + 1 + rows, cols]
        for k in range(1, taps):
            acc = acc + w_ref[k : k + 1, cols] * pad[8 - taps + 1 + k : 8 - taps + 1 + k + rows, cols]
        sig = jax.nn.sigmoid(acc)
        u = (acc * sig).astype(BF16)
        u_ref[:, cols] = u
        slope_ref[:, cols] = sig * (1.0 + acc * (1.0 - sig))
        return u

    bq = activate(pl.ds(channels, LANES)).astype(F32).T.astype(BF16)
    b_t = jnp.concatenate([bq[:BLOCK]] * 2, axis=1)
    q_t = jnp.concatenate([bq[BLOCK:]] * 2, axis=1)
    per_half = channels // 2 // LANES

    @pl.loop(0, channels // LANES)
    def _(j):
        cols = pl.ds(pl.multiple_of(j * LANES, LANES), LANES)
        side = j // per_half
        out = pl.ds(pl.multiple_of((j % per_half) * LANES, LANES), LANES)
        x = activate(cols).astype(F32)
        hot = one_hot(2 * heads, heads, 2 * j, LANES, BLOCK)
        spread = dot(facs[...], hot)
        fac_ref[side, :, out] = dot(small, hot)
        end_ref[side, :, out] = dot(b_t, jnp.concatenate(split2(x * spread[:rows]), axis=0))
        g = g_ref[:, cols].astype(F32)
        for level in range(far):
            inner = g * spread[(1 + level) * rows : (2 + level) * rows]
            gf_ref[level, side, :, out] = dot(q_t, jnp.concatenate(split2(inner), axis=0))


def fenwick_kernel(
    far, end_ref, gf_ref, fac_ref, far_ref, grad_ref,
    up0, up0_in, up, up_in, cross_in, merge, merge_in, down, down_in, last, last_in,
    sems_s, sems_r, run, back,
):
    me = lax.axis_index("ctx")
    core = me & 1
    other = 1 - core
    peers = [at(me ^ (1 << level)) for level in range(far)]

    def copy(src, dst, kind, level, peer):
        made = pltpu.make_async_remote_copy(
            src, dst, sems_s.at[kind, level], sems_r.at[kind, level], peer, MESH
        )
        made.start()
        return made

    pending = []
    up0[...] = end_ref[...].astype(BF16)
    for level in range(1, far):
        merge[level - 1] = gf_ref[level, other].astype(BF16)
    greet(peers)
    merge_copy = copy(merge, merge_in, 0, 0, peers[0])
    up_copy = copy(up0, up0_in, 1, 0, peers[0])
    crosses = []

    def own_coef(level):
        return fac_ref[core, 2 * level : 2 * level + 1, :]

    def sib_coef(level):
        return fac_ref[core, 2 * level + 1 : 2 * level + 2, :]

    merge_copy.wait()
    pending_down = None
    for step in range(far - 1):
        level = far - 1 - step
        total = gf_ref[level, core] + merge_in[level - 1].astype(F32)
        if step > 0:
            pending_down.wait()
            back[...] = back[...] * own_coef(level + 1) if step > 1 else jnp.zeros_like(back)
            back[...] = back[...] + down_in[level].astype(F32)
            total = total + back[...] * sib_coef(level)
        down[level - 1] = total.astype(BF16)
        pending_down = copy(down.at[level - 1], down_in.at[level - 1], 2, level, peers[level])

        up_copy.wait()
        if step == 0:
            run[...] = end_ref[core] * own_coef(0) + up0_in[core].astype(F32) * sib_coef(0)
        else:
            crosses.append(copy(up_in.at[step - 1], cross_in.at[step - 1], 3, step, peers[0]))
            run[...] = run[...] * own_coef(step) + up_in[step - 1].astype(F32) * sib_coef(step)
        up[step] = run[...].astype(BF16)
        up_copy = copy(up.at[step], up_in.at[step], 1, step + 1, peers[step + 1])
    pending_down.wait()
    if far > 2:
        back[...] = back[...] * own_coef(1) + down_in[0].astype(F32)
    else:
        back[...] = down_in[0].astype(F32)
    last[core] = (gf_ref[0, core] + back[...] * sib_coef(0)).astype(BF16)
    last[other] = gf_ref[0, other].astype(BF16)
    last_copy = copy(last, last_in, 4, 0, peers[0])
    up_copy.wait()
    crosses.append(copy(up_in.at[far - 2], cross_in.at[far - 2], 3, far - 1, peers[0]))
    far_ref[0] = up0_in[...]
    for level in range(1, far):
        far_ref[level, core] = up_in[level - 1]
    last_copy.wait()
    grad_ref[core] = back[...] * own_coef(0) + last_in[core].astype(F32)
    grad_ref[other] = last_in[other].astype(F32)
    for level in range(1, far):
        crosses[level - 1].wait()
        far_ref[level, other] = cross_in[level - 1]


def exchange_states(far, end_state, grad_far, factors):
    half = end_state.shape
    piece = half[1:]
    vm = pl.BlockSpec(memory_space=pltpu.VMEM)
    stack = (far - 1,) + piece
    return pl.pallas_call(
        functools.partial(fenwick_kernel, far),
        out_shape=(
            jax.ShapeDtypeStruct((far,) + half, BF16),
            jax.ShapeDtypeStruct(half, F32),
        ),
        in_specs=[vm] * 3,
        out_specs=(vm, vm),
        scratch_shapes=[
            pltpu.VMEM(half, BF16),
            pltpu.VMEM(half, BF16),
            pltpu.VMEM(stack, BF16),
            pltpu.VMEM(stack, BF16),
            pltpu.VMEM(stack, BF16),
            pltpu.VMEM(stack, BF16),
            pltpu.VMEM(stack, BF16),
            pltpu.VMEM(stack, BF16),
            pltpu.VMEM(stack, BF16),
            pltpu.VMEM(half, BF16),
            pltpu.VMEM(half, BF16),
            pltpu.SemaphoreType.DMA((5, far)),
            pltpu.SemaphoreType.DMA((5, far)),
            pltpu.VMEM(piece, F32),
            pltpu.VMEM(piece, F32),
        ],
        compiler_params=pltpu.CompilerParams(
            collective_id=1, has_side_effects=True, vmem_limit_bytes=VMEM_LIMIT
        ),
    )(end_state, grad_far, factors)


def back_kernel(
    far, conv_ref, prior_ref, w_ref, decay_ref, lw_ref, g_ref, u_ref, slope_ref, fac_ref, far_ref, grad_ref,
    mixed_ref, gin_ref, glev_ref, tail_ref, head_ref, wpart_ref,
    pad, gp, facs, cum3, cum_rows, bias, scores, hotx, hotg, q_s, b2_s, ds_acc, dq_acc, db_acc,
):
    rows, channels = g_ref.shape
    heads = decay_ref.shape[0]
    taps = w_ref.shape[0]
    wide = 2 * rows
    fill_padded(pad, conv_ref, prior_ref)
    cum = running_decay(decay_ref)
    cum_rows[...] = cum.T
    cum3[...] = jnp.concatenate(split3(cum), axis=1)
    base = [lw_ref[0].T * level_scale(0), lw_ref[1].T * level_scale(1)]
    base += [jnp.exp(cum[rows - 1 : rows] - cum), jnp.exp(cum)]
    base += [lw_ref[2 + level].T * level_scale(2 + level) for level in range(far)]
    for idx, value in enumerate(base):
        facs[idx * rows : (idx + 1) * rows, :] = jnp.concatenate(split2(value), axis=1)
    first = iota((rows, wide), 0)
    second = iota((rows, wide), 1) % rows
    bias[0] = jnp.where(second <= first, 0.0, -1e30)
    bias[1] = jnp.where(first <= second, 0.0, -1e30)
    r, c = iota((wide, wide), 0), iota((wide, wide), 1)
    same = (r // rows) == (c % LANES) // BLOCK
    block1 = (r % rows) // BLOCK == 1
    hotg[...] = jnp.where(same, 1.0, 0.0).astype(BF16)
    hotx[...] = jnp.where(same & (block1 == (c < LANES)), 1.0, 0.0).astype(BF16)
    bq = u_ref[:, channels:]
    b, q = bq[:, :BLOCK], bq[:, BLOCK:]
    q_s[...] = q
    b2_s[...] = jnp.concatenate([b, b], axis=1)
    scores[0] = dot_nt(q, jnp.concatenate([b, b], axis=0))
    scores[1] = dot_nt(b, jnp.concatenate([q, q], axis=0))
    ds_acc[...] = jnp.zeros_like(ds_acc)
    dq_acc[...] = jnp.zeros_like(dq_acc)
    db_acc[...] = jnp.zeros_like(db_acc)
    glev_ref[...] = jnp.zeros_like(glev_ref)
    per_half = channels // 2 // LANES
    low = iota((rows, LANES), 0) < BLOCK

    @pl.loop(0, channels // LANES)
    def _(j):
        cols = pl.ds(pl.multiple_of(j * LANES, LANES), LANES)
        side = j // per_half
        part = pl.ds(pl.multiple_of((j % per_half) * LANES, LANES), LANES)
        x = u_ref[:, cols]
        g = g_ref[:, cols].astype(F32)
        spread = dot(facs[...], one_hot(2 * heads, heads, 2 * j, LANES, BLOCK))

        def fac(idx):
            return spread[idx * rows : (idx + 1) * rows]

        w0, w1 = fac(0), fac(1)
        col = dot(cum3[...], one_hot(3 * heads, heads, 2 * j, wide, rows))
        row = jnp.concatenate([cum_rows[pl.ds(2 * j, 1), :], cum_rows[pl.ds(2 * j + 1, 1), :]], axis=1)
        gap = col - row
        decay = jnp.exp(gap + bias[0])
        mix = (scores[0] * decay).astype(BF16)
        mix_t = (scores[1] * jnp.exp(bias[1] - gap)).astype(BF16)
        wx = jnp.concatenate([jnp.concatenate([x, x], axis=1)] * 2, axis=0) * hotx[...]
        res = dot(mix, wx)
        out0 = jnp.where(low, res[:, LANES:], res[:, :LANES])
        out1 = jnp.where(low, 0.0, res[:, LANES:])
        gz = (g * w0).astype(BF16)
        gh = (g * jnp.where(low, w0, w1)).astype(BF16)
        gg = jnp.concatenate([gz, gh], axis=1)
        ds_acc[...] += decay * dot_nt(gg, wx)
        res = dot(mix_t, jnp.concatenate([gg, gg], axis=0) * hotg[...])
        dx = jnp.where(low, res[:, LANES:], res[:, :LANES])

        mixed = w0 * out0 + w1 * out1
        products = [g * out0, g * out1]
        inner, states = [], []
        for level in range(far):
            state = far_ref[level, side, :, part]
            scale = fac(3) * fac_ref[side, 2 * far + level : 2 * far + level + 1, part]
            out = dot(q_s[...], state) * scale
            weight = fac(4 + level)
            mixed = mixed + weight * out
            products.append(g * out)
            inner.append((g * weight * scale).astype(BF16))
            states.append(state)
        mixed_ref[:, cols] = mixed.astype(BF16)
        dq_acc[...] += dot_nt(jnp.concatenate(inner, axis=1), jnp.concatenate(states, axis=1))
        pick = jnp.where(
            iota((heads, 2 * LANES), 0) == 2 * j + (iota((heads, 2 * LANES), 1) % LANES) // BLOCK, 1.0, 0.0
        ).astype(BF16)
        for level, product in enumerate(products):
            glev_ref[level] += dot_nt(pick, jnp.concatenate(split2(product), axis=1)) * level_scale(level)

        grad = grad_ref[side, :, part]
        hi, lo = split2(grad)
        key_decay = fac(2)
        dx = dx + key_decay * dot(b2_s[...], jnp.concatenate([hi, lo], axis=0))
        db_acc[...] += dot_nt((x.astype(F32) * key_decay).astype(BF16), hi)
        gp[0:rows, cols] = dx * slope_ref[:, cols]

    ds = ds_acc[:, :rows] + ds_acc[:, rows:]
    dq = dq_acc[...] + dot(ds.astype(BF16), b)
    db = db_acc[...] + dot(ds.T.astype(BF16), q)
    gp[0:rows, channels:] = jnp.concatenate([db, dq], axis=1) * slope_ref[:, channels:]
    gp[rows:, :] = jnp.zeros((8, gp.shape[1]), F32)
    head_ref[...] = gp[0:8, :]

    @pl.loop(0, gp.shape[1] // LANES)
    def _(j):
        cols = pl.ds(pl.multiple_of(j * LANES, LANES), LANES)
        grad = gp[0:rows, cols]
        acc = w_ref[taps - 1 : taps, cols] * grad
        sums = []
        for k in range(taps):
            shift = taps - 1 - k
            if shift:
                acc = acc + w_ref[k : k + 1, cols] * gp[shift : shift + rows, cols]
            sums.append(jnp.sum(pad[8 - shift : 8 - shift + rows, cols] * grad, axis=0, keepdims=True))
        gin_ref[:, cols] = acc.astype(BF16)
        tail_ref[:, cols] = acc[rows - 16 :]
        sums.append(jnp.zeros((8 - taps, LANES), F32))
        wpart_ref[:, cols] = jnp.concatenate(sums, axis=0)


def finish_kernel(n, digits, tail_ref, head_ref, wpart_ref, w_ref, out_ref, wsum_ref, lead, nxt, acc, slots, hs, hr, send, recv):
    me = lax.axis_index("ctx")
    taps = w_ref.shape[0]
    channels = w_ref.shape[1]
    width = acc.shape[2]
    skip = channels - width

    def packed(rows):
        return jnp.concatenate([rows[:4, :width], rows[:4, skip:]], axis=0)

    def unpacked(value):
        return jnp.concatenate([value[:4, :skip], value[4:]], axis=1)

    lead[...] = packed(head_ref[...])
    acc[0] = packed(wpart_ref[...])
    before, after = lax.rem(me + n - 1, n), lax.rem(me + 1, n)
    plan = []
    for shift, size in digits:
        digit = (me >> shift) & (size - 1)
        plan.append((digit, [me ^ (d << shift) for d in range(1, size)]))
    greet([at(before), at(after)] + [at(p) for _, peers in plan for p in peers])
    row_copy = pltpu.make_async_remote_copy(lead, nxt, hs, hr, at(before), MESH)
    row_copy.start()
    for stage, (digit, peers) in enumerate(plan):
        copies = []
        for d, peer in enumerate(peers):
            copy = pltpu.make_async_remote_copy(
                acc.at[stage], slots.at[stage, d], send.at[stage, d], recv.at[stage, d], at(peer), MESH
            )
            copy.start()
            copies.append(copy)
        if stage == 0:
            row_copy.wait()
            keep = jnp.where(me < n - 1, 1.0, 0.0)
            rows = unpacked(nxt[...]) * keep
            blank = jnp.zeros((8, channels), F32)
            joined = jnp.concatenate([blank, rows, blank[:4]], axis=0)
            fix = blank
            for k in range(taps - 1):
                shift = taps - 1 - k
                fix = fix + w_ref[k : k + 1, :] * joined[shift : shift + 8]
            out_ref[...] = (tail_ref[...] + jnp.concatenate([jnp.zeros_like(fix), fix], axis=0)).astype(BF16)
        for copy in copies:
            copy.wait()
        size = len(peers) + 1
        have = [acc[stage]] + [slots[stage, d] for d in range(size - 1)]
        if size == 2:
            total = have[0] + have[1]
        else:
            total = (have[0] + have[1]) + (have[2] + have[3])
        acc[stage + 1] = total
    wsum_ref[...] = unpacked(acc[len(plan)])[:taps]


def exchange_finish(n, tail, head, wpart, conv_weight):
    far = n.bit_length() - 1
    digits = []
    shift = 0
    while shift < far:
        bits = min(2, far - shift)
        digits.append((shift, 1 << bits))
        shift += bits
    channels = tail.shape[1]
    width = (channels // LANES + 1) // 2 * LANES
    vm = pl.BlockSpec(memory_space=pltpu.VMEM)
    return pl.pallas_call(
        functools.partial(finish_kernel, n, digits),
        out_shape=(
            jax.ShapeDtypeStruct((16, channels), BF16),
            jax.ShapeDtypeStruct(conv_weight.shape, F32),
        ),
        in_specs=[vm] * 4,
        out_specs=(vm, vm),
        scratch_shapes=[
            pltpu.VMEM((8, width), F32),
            pltpu.VMEM((8, width), F32),
            pltpu.VMEM((len(digits) + 1, 8, width), F32),
            pltpu.VMEM((len(digits), 3, 8, width), F32),
            pltpu.SemaphoreType.DMA,
            pltpu.SemaphoreType.DMA,
            pltpu.SemaphoreType.DMA((len(digits), 3)),
            pltpu.SemaphoreType.DMA((len(digits), 3)),
        ],
        compiler_params=pltpu.CompilerParams(
            collective_id=2, has_side_effects=True, vmem_limit_bytes=VMEM_LIMIT
        ),
    )(tail, head, wpart, conv_weight)


def body(conv_input, conv_weight, log_decay, level_weight, grad_out):
    n = lax.axis_size("ctx")
    far = n.bit_length() - 1
    rows, conv_ch = conv_input.shape
    channels = grad_out.shape[1]
    heads = log_decay.shape[0]
    vm = pl.BlockSpec(memory_space=pltpu.VMEM)
    params = pltpu.CompilerParams(vmem_limit_bytes=VMEM_LIMIT)
    shape = jax.ShapeDtypeStruct
    half = (2, BLOCK, channels // 2)
    fac_rows = (3 * far + 7) // 8 * 8
    prior, totals = exchange_edges(n, conv_input, log_decay)
    u_act, slope, end_state, grad_far, factors = pl.pallas_call(
        functools.partial(front_kernel, far),
        out_shape=(
            shape((rows, conv_ch), BF16),
            shape((rows, conv_ch), F32),
            shape(half, F32),
            shape((far,) + half, F32),
            shape((2, fac_rows, channels // 2), F32),
        ),
        in_specs=[vm] * 7,
        out_specs=(vm,) * 5,
        scratch_shapes=[
            pltpu.VMEM((rows + 8, conv_ch), F32),
            pltpu.VMEM(((1 + far) * rows, 2 * heads), BF16),
        ],
        compiler_params=params,
    )(conv_input, prior, conv_weight, log_decay, level_weight, grad_out, totals)
    far_states, grad_end = exchange_states(far, end_state, grad_far, factors)
    mixed, grad_input, grad_level, tail, head, wpart = pl.pallas_call(
        functools.partial(back_kernel, far),
        out_shape=(
            shape((rows, channels), BF16),
            shape((rows, conv_ch), BF16),
            shape(level_weight.shape, F32),
            shape((16, conv_ch), F32),
            shape((8, conv_ch), F32),
            shape((8, conv_ch), F32),
        ),
        in_specs=[vm] * 11,
        out_specs=(vm,) * 6,
        scratch_shapes=[
            pltpu.VMEM((rows + 8, conv_ch), F32),
            pltpu.VMEM((rows + 8, conv_ch), F32),
            pltpu.VMEM(((4 + far) * rows, 2 * heads), BF16),
            pltpu.VMEM((rows, 3 * heads), BF16),
            pltpu.VMEM((heads, rows), F32),
            pltpu.VMEM((2, rows, 2 * rows), F32),
            pltpu.VMEM((2, rows, 2 * rows), F32),
            pltpu.VMEM((2 * rows, 2 * rows), BF16),
            pltpu.VMEM((2 * rows, 2 * rows), BF16),
            pltpu.VMEM((rows, BLOCK), BF16),
            pltpu.VMEM((rows, 2 * BLOCK), BF16),
            pltpu.VMEM((rows, 2 * rows), F32),
            pltpu.VMEM((rows, BLOCK), F32),
            pltpu.VMEM((rows, BLOCK), F32),
        ],
        compiler_params=params,
    )(
        conv_input, prior, conv_weight, log_decay, level_weight, grad_out,
        u_act, slope, factors, far_states, grad_end,
    )
    tail_rows, weight_grad = exchange_finish(n, tail, head, wpart, conv_weight)
    grad_input = lax.dynamic_update_slice(grad_input, tail_rows, (rows - 16, 0))
    return (mixed, grad_input, grad_level, weight_grad)


def solution(mesh):
    in_specs = (
        P(("groups", "ctx"), None),
        P(),
        P(None, ("groups", "ctx")),
        P(None, None, ("groups", "ctx")),
        P(("groups", "ctx"), None),
    )
    out_specs = (
        P(("groups", "ctx"), None),
        P(("groups", "ctx"), None),
        P(None, None, ("groups", "ctx")),
        P("groups", None),
    )
    return jax.shard_map(body, mesh=mesh, in_specs=in_specs, out_specs=out_specs, check_vma=False)
```

```python
import functools

import jax
import jax.numpy as jnp
from jax import lax
from jax.experimental import pallas as pl
from jax.experimental.pallas import tpu as pltpu
from jax.sharding import PartitionSpec as P

BLOCK = 64
LANES = 128
MESH = pl.DeviceIdType.MESH
HIGH = lax.Precision.HIGHEST
F32 = jnp.float32
BF16 = jnp.bfloat16
VMEM_LIMIT = 56 * 1024 * 1024


def level_scale(level_idx):
    if level_idx == 0:
        return BLOCK**-0.5
    return (BLOCK * 2 ** (level_idx - 1)) ** -0.5


def dot(a, b):
    return jnp.dot(a, b, preferred_element_type=F32)


def dot_nt(a, b):
    return lax.dot_general(a, b, (((1,), (1,)), ((), ())), preferred_element_type=F32)


def split2(v):
    hi = v.astype(BF16)
    return hi, (v - hi.astype(F32)).astype(BF16)


def split3(v):
    hi = v.astype(BF16)
    rest = v - hi.astype(F32)
    mid = rest.astype(BF16)
    return hi, mid, (rest - mid.astype(F32)).astype(BF16)


def iota(shape, axis):
    return lax.broadcasted_iota(jnp.int32, shape, axis)


def one_hot(rows, heads, first, lanes, width):
    return jnp.where(
        iota((rows, lanes), 0) % heads == first + iota((rows, lanes), 1) // width, 1.0, 0.0
    ).astype(BF16)


def greet(peers):
    barrier = pltpu.get_barrier_semaphore()
    for peer in peers:
        pl.semaphore_signal(barrier, inc=1, device_id=peer, device_id_type=MESH)
    pl.semaphore_wait(barrier, len(peers))


def at(peer):
    return (lax.axis_index("groups"), peer)


def edge_kernel(n, conv_ref, decay_ref, prior_ref, totals_ref, mine, slots, rows, send, recv, rsend, rrecv):
    me = lax.axis_index("ctx")
    peers = [lax.rem(me + d, n) for d in range(1, n)]
    heads = decay_ref.shape[0]
    mine[...] = jnp.zeros_like(mine)
    mine[:, :heads] = lax.dot_general(
        jnp.ones((8, decay_ref.shape[1]), F32),
        decay_ref[...],
        (((1,), (1,)), ((), ())),
        precision=HIGH,
        preferred_element_type=F32,
    )
    greet([at(p) for p in peers])
    copies = []
    count = conv_ref.shape[0]
    row_copy = pltpu.make_async_remote_copy(
        conv_ref.at[pl.ds(count - 16, 16), :], rows, rsend, rrecv, at(peers[0]), MESH
    )
    row_copy.start()
    for d in range(1, n):
        copy = pltpu.make_async_remote_copy(
            mine, slots.at[d - 1], send.at[d - 1], recv.at[d - 1], at(peers[d - 1]), MESH
        )
        copy.start()
        copies.append(copy)
    totals_ref[me] = mine[...]
    for d in range(1, n):
        copies[d - 1].wait()
        totals_ref[lax.rem(me - d + n, n)] = slots[d - 1]
    row_copy.wait()
    keep = jnp.where(me > 0, 1.0, 0.0)
    prior_ref[...] = (rows[...].astype(F32) * keep).astype(BF16)


def exchange_edges(n, conv_input, log_decay):
    channels = conv_input.shape[1]
    vm = pl.BlockSpec(memory_space=pltpu.VMEM)
    return pl.pallas_call(
        functools.partial(edge_kernel, n),
        out_shape=(
            jax.ShapeDtypeStruct((16, channels), BF16),
            jax.ShapeDtypeStruct((n, 8, LANES), F32),
        ),
        in_specs=[pl.BlockSpec(memory_space=pl.ANY), vm],
        out_specs=(vm, vm),
        scratch_shapes=[
            pltpu.VMEM((8, LANES), F32),
            pltpu.VMEM((n - 1, 8, LANES), F32),
            pltpu.VMEM((16, channels), BF16),
            pltpu.SemaphoreType.DMA((n - 1,)),
            pltpu.SemaphoreType.DMA((n - 1,)),
            pltpu.SemaphoreType.DMA,
            pltpu.SemaphoreType.DMA,
        ],
        compiler_params=pltpu.CompilerParams(
            collective_id=0, has_side_effects=True, vmem_limit_bytes=VMEM_LIMIT
        ),
    )(conv_input, log_decay)


def fill_padded(pad, conv_ref, prior_ref):
    pad[0:8, :] = prior_ref[...].astype(F32)[8:16]
    pad[8:, :] = conv_ref[...].astype(F32)


def running_decay(decay_ref):
    rows = decay_ref.shape[1]
    lower = jnp.where(iota((rows, rows), 0) >= iota((rows, rows), 1), 1.0, 0.0)
    by_token = jnp.dot(lower, decay_ref[...].T, precision=HIGH, preferred_element_type=F32)
    return by_token


def front_kernel(
    far, conv_ref, prior_ref, w_ref, decay_ref, lw_ref, g_ref, totals_ref,
    u_ref, slope_ref, end_ref, gf_ref, fac_ref, pad, facs,
):
    me = lax.axis_index("ctx")
    rows, channels = g_ref.shape
    heads = decay_ref.shape[0]
    taps = w_ref.shape[0]
    fill_padded(pad, conv_ref, prior_ref)
    totals = totals_ref[...][:, 0, :heads]
    spans = iota(totals.shape, 0)

    def span(lo, hi):
        return jnp.sum(jnp.where((spans >= lo) & (spans < hi), totals, 0.0), axis=0, keepdims=True)

    own, pre = [], []
    for level in range(far):
        half = me >> level
        upper = (half & 1) == 1
        start = half << level
        sib = (half ^ 1) << level
        size = 1 << level
        own.append(jnp.exp(jnp.where(upper, 0.0, 1.0) * span(sib, sib + size)))
        own.append(jnp.exp(jnp.where(upper, 1.0, 0.0) * span(start, start + size)))
        pre.append(jnp.where(upper, 1.0, 0.0) * jnp.exp(span(start, me)))
    count = fac_ref.shape[1]
    stack = own + pre
    if count > len(stack):
        stack.append(jnp.zeros((count - len(stack), heads), F32))
    small = jnp.concatenate(split2(jnp.concatenate(stack, axis=0)), axis=1)

    cum = running_decay(decay_ref)
    in_device = jnp.exp(cum)
    base = [jnp.exp(cum[rows - 1 : rows] - cum)]
    for level in range(far):
        base.append(in_device * lw_ref[2 + level].T * (level_scale(2 + level) * pre[level]))
    for idx, value in enumerate(base):
        facs[idx * rows : (idx + 1) * rows, :] = jnp.concatenate(split2(value), axis=1)

    def activate(cols):
        acc = w_ref[0:1, cols] * pad[8 - taps + 1 : 8 - taps + 1 + rows, cols]
        for k in range(1, taps):
            acc = acc + w_ref[k : k + 1, cols] * pad[8 - taps + 1 + k : 8 - taps + 1 + k + rows, cols]
        sig = jax.nn.sigmoid(acc)
        u = (acc * sig).astype(BF16)
        u_ref[:, cols] = u
        slope_ref[:, cols] = sig * (1.0 + acc * (1.0 - sig))
        return u

    bq = activate(pl.ds(channels, LANES)).astype(F32).T.astype(BF16)
    b_t = jnp.concatenate([bq[:BLOCK]] * 2, axis=1)
    q_t = jnp.concatenate([bq[BLOCK:]] * 2, axis=1)
    per_half = channels // 2 // LANES

    @pl.loop(0, channels // LANES)
    def _(j):
        cols = pl.ds(pl.multiple_of(j * LANES, LANES), LANES)
        side = j // per_half
        out = pl.ds(pl.multiple_of((j % per_half) * LANES, LANES), LANES)
        x = activate(cols).astype(F32)
        hot = one_hot(2 * heads, heads, 2 * j, LANES, BLOCK)
        spread = dot(facs[...], hot)
        fac_ref[side, :, out] = dot(small, hot)
        end_ref[side, :, out] = dot(b_t, jnp.concatenate(split2(x * spread[:rows]), axis=0))
        g = g_ref[:, cols].astype(F32)
        for level in range(far):
            inner = g * spread[(1 + level) * rows : (2 + level) * rows]
            gf_ref[level, side, :, out] = dot(q_t, jnp.concatenate(split2(inner), axis=0))


def near_setup(decay_ref, lw_ref, u_ref, glev_ref, facs, cum3, cum_rows, bias, scores, hotx, hotg, ds_acc):
    rows = decay_ref.shape[1]
    wide = 2 * rows
    cum = running_decay(decay_ref)
    cum_rows[...] = cum.T
    cum3[...] = jnp.concatenate(split3(cum), axis=1)
    for level in range(2):
        value = lw_ref[level].T * level_scale(level)
        facs[level * rows : (level + 1) * rows, :] = jnp.concatenate(split2(value), axis=1)
    first = iota((rows, wide), 0)
    second = iota((rows, wide), 1) % rows
    bias[0] = jnp.where(second <= first, 0.0, -1e30)
    bias[1] = jnp.where(first <= second, 0.0, -1e30)
    r, c = iota((wide, wide), 0), iota((wide, wide), 1)
    same = (r // rows) == (c % LANES) // BLOCK
    block1 = (r % rows) // BLOCK == 1
    hotg[...] = jnp.where(same, 1.0, 0.0).astype(BF16)
    hotx[...] = jnp.where(same & (block1 == (c < LANES)), 1.0, 0.0).astype(BF16)
    bq = u_ref[:, u_ref.shape[1] - LANES :]
    b, q = bq[:, :BLOCK], bq[:, BLOCK:]
    scores[0] = dot_nt(q, jnp.concatenate([b, b], axis=0))
    scores[1] = dot_nt(b, jnp.concatenate([q, q], axis=0))
    ds_acc[...] = jnp.zeros_like(ds_acc)
    glev_ref[...] = jnp.zeros_like(glev_ref)


def head_pick(heads, j):
    lanes = iota((heads, 2 * LANES), 1) % LANES
    return jnp.where(iota((heads, 2 * LANES), 0) == 2 * j + lanes // BLOCK, 1.0, 0.0).astype(BF16)


def near_pair(j, g_ref, u_ref, mixed_ref, dx_ref, glev_ref, facs, cum3, cum_rows, bias, scores, hotx, hotg, ds_acc):
    heads, rows = cum_rows.shape
    wide = 2 * rows
    low = iota((rows, LANES), 0) < BLOCK
    cols = pl.ds(pl.multiple_of(j * LANES, LANES), LANES)
    x = u_ref[:, cols]
    g = g_ref[:, cols].astype(F32)
    spread = dot(facs[...], one_hot(2 * heads, heads, 2 * j, LANES, BLOCK))
    w0, w1 = spread[:rows], spread[rows:]
    col = dot(cum3[...], one_hot(3 * heads, heads, 2 * j, wide, rows))
    row = jnp.concatenate([cum_rows[pl.ds(2 * j, 1), :], cum_rows[pl.ds(2 * j + 1, 1), :]], axis=1)
    gap = col - row
    decay = jnp.exp(gap + bias[0])
    mix = (scores[0] * decay).astype(BF16)
    mix_t = (scores[1] * jnp.exp(bias[1] - gap)).astype(BF16)
    wx = jnp.concatenate([jnp.concatenate([x, x], axis=1)] * 2, axis=0) * hotx[...]
    res = dot(mix, wx)
    out0 = jnp.where(low, res[:, LANES:], res[:, :LANES])
    out1 = jnp.where(low, 0.0, res[:, LANES:])
    gz = (g * w0).astype(BF16)
    gh = (g * jnp.where(low, w0, w1)).astype(BF16)
    gg = jnp.concatenate([gz, gh], axis=1)
    ds_acc[...] += decay * dot_nt(gg, wx)
    res = dot(mix_t, jnp.concatenate([gg, gg], axis=0) * hotg[...])
    dx_ref[:, cols] = jnp.where(low, res[:, LANES:], res[:, :LANES])
    mixed_ref[:, cols] = w0 * out0 + w1 * out1
    pick = head_pick(heads, j)
    for level, out in enumerate((out0, out1)):
        glev_ref[level] += dot_nt(pick, jnp.concatenate(split2(g * out), axis=1)) * level_scale(level)


def fenwick_kernel(
    far, end_ref, gf_ref, fac_ref, decay_ref, lw_ref, g_ref, u_ref,
    far_ref, grad_ref, mixed_ref, dx_ref, glev_ref, dbq_ref,
    facs, cum3, cum_rows, bias, scores, hotx, hotg, ds_acc,
    up0, up0_in, up, up_in, cross_in, merge, merge_in, down, down_in, last, last_in,
    sems_s, sems_r, run, back,
):
    me = lax.axis_index("ctx")
    core = me & 1
    other = 1 - core
    peers = [at(me ^ (1 << level)) for level in range(far)]

    def copy(src, dst, kind, level, peer):
        made = pltpu.make_async_remote_copy(
            src, dst, sems_s.at[kind, level], sems_r.at[kind, level], peer, MESH
        )
        made.start()
        return made

    pending = []
    up0[...] = end_ref[...].astype(BF16)
    for level in range(1, far):
        merge[level - 1] = gf_ref[level, other].astype(BF16)
    greet(peers)
    merge_copy = copy(merge, merge_in, 0, 0, peers[0])
    up_copy = copy(up0, up0_in, 1, 0, peers[0])
    crosses = []

    def own_coef(level):
        return fac_ref[core, 2 * level : 2 * level + 1, :]

    def sib_coef(level):
        return fac_ref[core, 2 * level + 1 : 2 * level + 2, :]

    near_setup(decay_ref, lw_ref, u_ref, glev_ref, facs, cum3, cum_rows, bias, scores, hotx, hotg, ds_acc)
    pairs = g_ref.shape[1] // LANES
    cuts = [0, 1] + [1 + (pairs - 1) * (step + 1) // (far - 1) for step in range(far - 1)]

    def near_part(lo, hi):
        @pl.loop(lo, hi)
        def _(j):
            near_pair(
                j, g_ref, u_ref, mixed_ref, dx_ref, glev_ref, facs, cum3, cum_rows, bias, scores, hotx, hotg, ds_acc
            )

    near_part(cuts[0], cuts[1])
    merge_copy.wait()
    pending_down = None
    for step in range(far - 1):
        level = far - 1 - step
        total = gf_ref[level, core] + merge_in[level - 1].astype(F32)
        if step > 0:
            pending_down.wait()
            back[...] = back[...] * own_coef(level + 1) if step > 1 else jnp.zeros_like(back)
            back[...] = back[...] + down_in[level].astype(F32)
            total = total + back[...] * sib_coef(level)
        down[level - 1] = total.astype(BF16)
        pending_down = copy(down.at[level - 1], down_in.at[level - 1], 2, level, peers[level])

        up_copy.wait()
        if step == 0:
            run[...] = end_ref[core] * own_coef(0) + up0_in[core].astype(F32) * sib_coef(0)
        else:
            crosses.append(copy(up_in.at[step - 1], cross_in.at[step - 1], 3, step, peers[0]))
            run[...] = run[...] * own_coef(step) + up_in[step - 1].astype(F32) * sib_coef(step)
        up[step] = run[...].astype(BF16)
        up_copy = copy(up.at[step], up_in.at[step], 1, step + 1, peers[step + 1])
        near_part(cuts[step + 1], cuts[step + 2])
    pending_down.wait()
    if far > 2:
        back[...] = back[...] * own_coef(1) + down_in[0].astype(F32)
    else:
        back[...] = down_in[0].astype(F32)
    last[core] = (gf_ref[0, core] + back[...] * sib_coef(0)).astype(BF16)
    last[other] = gf_ref[0, other].astype(BF16)
    last_copy = copy(last, last_in, 4, 0, peers[0])
    rows = decay_ref.shape[1]
    bq = u_ref[:, u_ref.shape[1] - LANES :]
    ds = ds_acc[:, :rows] + ds_acc[:, rows:]
    dq = dot(ds.astype(BF16), bq[:, :BLOCK])
    db = dot(ds.T.astype(BF16), bq[:, BLOCK:])
    dbq_ref[...] = jnp.concatenate([db, dq], axis=1)
    up_copy.wait()
    crosses.append(copy(up_in.at[far - 2], cross_in.at[far - 2], 3, far - 1, peers[0]))
    far_ref[0] = up0_in[...]
    for level in range(1, far):
        far_ref[level, core] = up_in[level - 1]
    last_copy.wait()
    grad_ref[core] = back[...] * own_coef(0) + last_in[core].astype(F32)
    grad_ref[other] = last_in[other].astype(F32)
    for level in range(1, far):
        crosses[level - 1].wait()
        far_ref[level, other] = cross_in[level - 1]


def exchange_states(far, end_state, grad_far, factors, log_decay, level_weight, grad_out, u_act):
    half = end_state.shape
    piece = half[1:]
    vm = pl.BlockSpec(memory_space=pltpu.VMEM)
    stack = (far - 1,) + piece
    heads, rows = log_decay.shape
    channels = grad_out.shape[1]
    return pl.pallas_call(
        functools.partial(fenwick_kernel, far),
        out_shape=(
            jax.ShapeDtypeStruct((far,) + half, BF16),
            jax.ShapeDtypeStruct(half, F32),
            jax.ShapeDtypeStruct((rows, channels), F32),
            jax.ShapeDtypeStruct((rows, channels), F32),
            jax.ShapeDtypeStruct((2, heads, rows), F32),
            jax.ShapeDtypeStruct((rows, LANES), F32),
        ),
        in_specs=[vm] * 7,
        out_specs=(vm,) * 6,
        scratch_shapes=[
            pltpu.VMEM((2 * rows, 2 * heads), BF16),
            pltpu.VMEM((rows, 3 * heads), BF16),
            pltpu.VMEM((heads, rows), F32),
            pltpu.VMEM((2, rows, 2 * rows), F32),
            pltpu.VMEM((2, rows, 2 * rows), F32),
            pltpu.VMEM((2 * rows, 2 * rows), BF16),
            pltpu.VMEM((2 * rows, 2 * rows), BF16),
            pltpu.VMEM((rows, 2 * rows), F32),
            pltpu.VMEM(half, BF16),
            pltpu.VMEM(half, BF16),
            pltpu.VMEM(stack, BF16),
            pltpu.VMEM(stack, BF16),
            pltpu.VMEM(stack, BF16),
            pltpu.VMEM(stack, BF16),
            pltpu.VMEM(stack, BF16),
            pltpu.VMEM(stack, BF16),
            pltpu.VMEM(stack, BF16),
            pltpu.VMEM(half, BF16),
            pltpu.VMEM(half, BF16),
            pltpu.SemaphoreType.DMA((5, far)),
            pltpu.SemaphoreType.DMA((5, far)),
            pltpu.VMEM(piece, F32),
            pltpu.VMEM(piece, F32),
        ],
        compiler_params=pltpu.CompilerParams(
            collective_id=1, has_side_effects=True, vmem_limit_bytes=VMEM_LIMIT
        ),
    )(end_state, grad_far, factors, log_decay, level_weight, grad_out, u_act)


def back_kernel(
    far, conv_ref, prior_ref, w_ref, decay_ref, lw_ref, g_ref, u_ref, slope_ref, fac_ref, far_ref, grad_ref,
    near_ref, dx_ref, nlev_ref, dbq_ref,
    mixed_ref, gin_ref, glev_ref, tail_ref, head_ref, wpart_ref,
    pad, gp, facs, q_s, b2_s, dq_acc, db_acc,
):
    rows, channels = g_ref.shape
    heads = decay_ref.shape[0]
    taps = w_ref.shape[0]
    fill_padded(pad, conv_ref, prior_ref)
    cum = running_decay(decay_ref)
    base = [jnp.exp(cum[rows - 1 : rows] - cum), jnp.exp(cum)]
    base += [lw_ref[2 + level].T * level_scale(2 + level) for level in range(far)]
    for idx, value in enumerate(base):
        facs[idx * rows : (idx + 1) * rows, :] = jnp.concatenate(split2(value), axis=1)
    bq = u_ref[:, channels:]
    q_s[...] = bq[:, BLOCK:]
    b2_s[...] = jnp.concatenate([bq[:, :BLOCK]] * 2, axis=1)
    dq_acc[...] = jnp.zeros_like(dq_acc)
    db_acc[...] = jnp.zeros_like(db_acc)
    glev_ref[...] = jnp.zeros_like(glev_ref)
    glev_ref[0:2] = nlev_ref[...]
    per_half = channels // 2 // LANES

    @pl.loop(0, channels // LANES)
    def _(j):
        cols = pl.ds(pl.multiple_of(j * LANES, LANES), LANES)
        side = j // per_half
        part = pl.ds(pl.multiple_of((j % per_half) * LANES, LANES), LANES)
        x = u_ref[:, cols]
        g = g_ref[:, cols].astype(F32)
        spread = dot(facs[...], one_hot(2 * heads, heads, 2 * j, LANES, BLOCK))

        def fac(idx):
            return spread[idx * rows : (idx + 1) * rows]

        mixed = near_ref[:, cols]
        products, inner, states = [], [], []
        for level in range(far):
            state = far_ref[level, side, :, part]
            scale = fac(1) * fac_ref[side, 2 * far + level : 2 * far + level + 1, part]
            out = dot(q_s[...], state) * scale
            weight = fac(2 + level)
            mixed = mixed + weight * out
            products.append(g * out)
            inner.append((g * weight * scale).astype(BF16))
            states.append(state)
        mixed_ref[:, cols] = mixed.astype(BF16)
        dq_acc[...] += dot_nt(jnp.concatenate(inner, axis=1), jnp.concatenate(states, axis=1))
        pick = head_pick(heads, j)
        for level, product in enumerate(products):
            sums = dot_nt(pick, jnp.concatenate(split2(product), axis=1))
            glev_ref[2 + level] += sums * level_scale(2 + level)

        grad = grad_ref[side, :, part]
        hi, lo = split2(grad)
        key_decay = fac(0)
        dx = dx_ref[:, cols] + key_decay * dot(b2_s[...], jnp.concatenate([hi, lo], axis=0))
        db_acc[...] += dot_nt((x.astype(F32) * key_decay).astype(BF16), hi)
        gp[0:rows, cols] = dx * slope_ref[:, cols]

    dbq = dbq_ref[...] + jnp.concatenate([db_acc[...], dq_acc[...]], axis=1)
    gp[0:rows, channels:] = dbq * slope_ref[:, channels:]
    gp[rows:, :] = jnp.zeros((8, gp.shape[1]), F32)
    head_ref[...] = gp[0:8, :]

    @pl.loop(0, gp.shape[1] // LANES)
    def _(j):
        cols = pl.ds(pl.multiple_of(j * LANES, LANES), LANES)
        grad = gp[0:rows, cols]
        acc = w_ref[taps - 1 : taps, cols] * grad
        sums = []
        for k in range(taps):
            shift = taps - 1 - k
            if shift:
                acc = acc + w_ref[k : k + 1, cols] * gp[shift : shift + rows, cols]
            sums.append(jnp.sum(pad[8 - shift : 8 - shift + rows, cols] * grad, axis=0, keepdims=True))
        gin_ref[:, cols] = acc.astype(BF16)
        tail_ref[:, cols] = acc[rows - 16 :]
        sums.append(jnp.zeros((8 - taps, LANES), F32))
        wpart_ref[:, cols] = jnp.concatenate(sums, axis=0)


def finish_kernel(n, digits, tail_ref, head_ref, wpart_ref, w_ref, out_ref, wsum_ref, lead, nxt, acc, slots, hs, hr, send, recv):
    me = lax.axis_index("ctx")
    taps = w_ref.shape[0]
    channels = w_ref.shape[1]
    width = acc.shape[2]
    skip = channels - width

    def packed(rows):
        return jnp.concatenate([rows[:4, :width], rows[:4, skip:]], axis=0)

    def unpacked(value):
        return jnp.concatenate([value[:4, :skip], value[4:]], axis=1)

    lead[...] = packed(head_ref[...])
    acc[0] = packed(wpart_ref[...])
    before, after = lax.rem(me + n - 1, n), lax.rem(me + 1, n)
    plan = []
    for shift, size in digits:
        digit = (me >> shift) & (size - 1)
        plan.append((digit, [me ^ (d << shift) for d in range(1, size)]))
    greet([at(before), at(after)] + [at(p) for _, peers in plan for p in peers])
    row_copy = pltpu.make_async_remote_copy(lead, nxt, hs, hr, at(before), MESH)
    row_copy.start()
    for stage, (digit, peers) in enumerate(plan):
        copies = []
        for d, peer in enumerate(peers):
            copy = pltpu.make_async_remote_copy(
                acc.at[stage], slots.at[stage, d], send.at[stage, d], recv.at[stage, d], at(peer), MESH
            )
            copy.start()
            copies.append(copy)
        if stage == 0:
            row_copy.wait()
            keep = jnp.where(me < n - 1, 1.0, 0.0)
            rows = unpacked(nxt[...]) * keep
            blank = jnp.zeros((8, channels), F32)
            joined = jnp.concatenate([blank, rows, blank[:4]], axis=0)
            fix = blank
            for k in range(taps - 1):
                shift = taps - 1 - k
                fix = fix + w_ref[k : k + 1, :] * joined[shift : shift + 8]
            out_ref[...] = (tail_ref[...] + jnp.concatenate([jnp.zeros_like(fix), fix], axis=0)).astype(BF16)
        for copy in copies:
            copy.wait()
        size = len(peers) + 1
        have = [acc[stage]] + [slots[stage, d] for d in range(size - 1)]
        if size == 2:
            total = have[0] + have[1]
        else:
            total = (have[0] + have[1]) + (have[2] + have[3])
        acc[stage + 1] = total
    wsum_ref[...] = unpacked(acc[len(plan)])[:taps]


def exchange_finish(n, tail, head, wpart, conv_weight):
    far = n.bit_length() - 1
    digits = []
    shift = 0
    while shift < far:
        bits = min(2, far - shift)
        digits.append((shift, 1 << bits))
        shift += bits
    channels = tail.shape[1]
    width = (channels // LANES + 1) // 2 * LANES
    vm = pl.BlockSpec(memory_space=pltpu.VMEM)
    return pl.pallas_call(
        functools.partial(finish_kernel, n, digits),
        out_shape=(
            jax.ShapeDtypeStruct((16, channels), BF16),
            jax.ShapeDtypeStruct(conv_weight.shape, F32),
        ),
        in_specs=[vm] * 4,
        out_specs=(vm, vm),
        scratch_shapes=[
            pltpu.VMEM((8, width), F32),
            pltpu.VMEM((8, width), F32),
            pltpu.VMEM((len(digits) + 1, 8, width), F32),
            pltpu.VMEM((len(digits), 3, 8, width), F32),
            pltpu.SemaphoreType.DMA,
            pltpu.SemaphoreType.DMA,
            pltpu.SemaphoreType.DMA((len(digits), 3)),
            pltpu.SemaphoreType.DMA((len(digits), 3)),
        ],
        compiler_params=pltpu.CompilerParams(
            collective_id=2, has_side_effects=True, vmem_limit_bytes=VMEM_LIMIT
        ),
    )(tail, head, wpart, conv_weight)


def body(conv_input, conv_weight, log_decay, level_weight, grad_out):
    n = lax.axis_size("ctx")
    far = n.bit_length() - 1
    rows, conv_ch = conv_input.shape
    channels = grad_out.shape[1]
    heads = log_decay.shape[0]
    vm = pl.BlockSpec(memory_space=pltpu.VMEM)
    params = pltpu.CompilerParams(vmem_limit_bytes=VMEM_LIMIT)
    shape = jax.ShapeDtypeStruct
    half = (2, BLOCK, channels // 2)
    fac_rows = (3 * far + 7) // 8 * 8
    prior, totals = exchange_edges(n, conv_input, log_decay)
    u_act, slope, end_state, grad_far, factors = pl.pallas_call(
        functools.partial(front_kernel, far),
        out_shape=(
            shape((rows, conv_ch), BF16),
            shape((rows, conv_ch), F32),
            shape(half, F32),
            shape((far,) + half, F32),
            shape((2, fac_rows, channels // 2), F32),
        ),
        in_specs=[vm] * 7,
        out_specs=(vm,) * 5,
        scratch_shapes=[
            pltpu.VMEM((rows + 8, conv_ch), F32),
            pltpu.VMEM(((1 + far) * rows, 2 * heads), BF16),
        ],
        compiler_params=params,
    )(conv_input, prior, conv_weight, log_decay, level_weight, grad_out, totals)
    far_states, grad_end, *near = exchange_states(
        far, end_state, grad_far, factors, log_decay, level_weight, grad_out, u_act
    )
    mixed, grad_input, grad_level, tail, head, wpart = pl.pallas_call(
        functools.partial(back_kernel, far),
        out_shape=(
            shape((rows, channels), BF16),
            shape((rows, conv_ch), BF16),
            shape(level_weight.shape, F32),
            shape((16, conv_ch), F32),
            shape((8, conv_ch), F32),
            shape((8, conv_ch), F32),
        ),
        in_specs=[vm] * 15,
        out_specs=(vm,) * 6,
        scratch_shapes=[
            pltpu.VMEM((rows + 8, conv_ch), F32),
            pltpu.VMEM((rows + 8, conv_ch), F32),
            pltpu.VMEM(((2 + far) * rows, 2 * heads), BF16),
            pltpu.VMEM((rows, BLOCK), BF16),
            pltpu.VMEM((rows, 2 * BLOCK), BF16),
            pltpu.VMEM((rows, BLOCK), F32),
            pltpu.VMEM((rows, BLOCK), F32),
        ],
        compiler_params=params,
    )(
        conv_input, prior, conv_weight, log_decay, level_weight, grad_out,
        u_act, slope, factors, far_states, grad_end, *near,
    )
    tail_rows, weight_grad = exchange_finish(n, tail, head, wpart, conv_weight)
    grad_input = lax.dynamic_update_slice(grad_input, tail_rows, (rows - 16, 0))
    return (mixed, grad_input, grad_level, weight_grad)


def solution(mesh):
    in_specs = (
        P(("groups", "ctx"), None),
        P(),
        P(None, ("groups", "ctx")),
        P(None, None, ("groups", "ctx")),
        P(("groups", "ctx"), None),
    )
    out_specs = (
        P(("groups", "ctx"), None),
        P(("groups", "ctx"), None),
        P(None, None, ("groups", "ctx")),
        P("groups", None),
    )
    return jax.shard_map(body, mesh=mesh, in_specs=in_specs, out_specs=out_specs, check_vma=False)
```

```python
import functools

import jax
import jax.numpy as jnp
from jax import lax
from jax.experimental import pallas as pl
from jax.experimental.pallas import tpu as pltpu
from jax.sharding import PartitionSpec as P

BLOCK = 64
LANES = 128
MESH = pl.DeviceIdType.MESH
HIGH = lax.Precision.HIGHEST
F32 = jnp.float32
BF16 = jnp.bfloat16
VMEM_LIMIT = 56 * 1024 * 1024


def level_scale(level_idx):
    if level_idx == 0:
        return BLOCK**-0.5
    return (BLOCK * 2 ** (level_idx - 1)) ** -0.5


def dot(a, b):
    return jnp.dot(a, b, preferred_element_type=F32)


def dot_nt(a, b):
    return lax.dot_general(a, b, (((1,), (1,)), ((), ())), preferred_element_type=F32)


def split2(v):
    hi = v.astype(BF16)
    return hi, (v - hi.astype(F32)).astype(BF16)


def split3(v):
    hi = v.astype(BF16)
    rest = v - hi.astype(F32)
    mid = rest.astype(BF16)
    return hi, mid, (rest - mid.astype(F32)).astype(BF16)


def iota(shape, axis):
    return lax.broadcasted_iota(jnp.int32, shape, axis)


def one_hot(rows, heads, first, lanes, width):
    return jnp.where(
        iota((rows, lanes), 0) % heads == first + iota((rows, lanes), 1) // width, 1.0, 0.0
    ).astype(BF16)


def greet(peers):
    barrier = pltpu.get_barrier_semaphore()
    for peer in peers:
        pl.semaphore_signal(barrier, inc=1, device_id=peer, device_id_type=MESH)
    pl.semaphore_wait(barrier, len(peers))


def at(peer):
    return (lax.axis_index("groups"), peer)


def start_edges(n, conv_ref, decay_ref, prior_ref, totals_ref, mine, slots, rows, send, recv, rsend, rrecv):
    me = lax.axis_index("ctx")
    peers = [lax.rem(me + d, n) for d in range(1, n)]
    heads = decay_ref.shape[0]
    mine[...] = jnp.zeros_like(mine)
    mine[:, :heads] = lax.dot_general(
        jnp.ones((8, decay_ref.shape[1]), F32),
        decay_ref[...],
        (((1,), (1,)), ((), ())),
        precision=HIGH,
        preferred_element_type=F32,
    )
    greet([at(p) for p in peers])
    copies = []
    count = conv_ref.shape[0]
    row_copy = pltpu.make_async_remote_copy(
        conv_ref.at[pl.ds(count - 16, 16), :], rows, rsend, rrecv, at(peers[0]), MESH
    )
    row_copy.start()
    for d in range(1, n):
        copy = pltpu.make_async_remote_copy(
            mine, slots.at[d - 1], send.at[d - 1], recv.at[d - 1], at(peers[d - 1]), MESH
        )
        copy.start()
        copies.append(copy)
    totals_ref[me] = mine[...]

    def finish():
        for d in range(1, n):
            copies[d - 1].wait()
            totals_ref[lax.rem(me - d + n, n)] = slots[d - 1]
        row_copy.wait()
        keep = jnp.where(me > 0, 1.0, 0.0)
        prior_ref[...] = (rows[...].astype(F32) * keep).astype(BF16)

    return finish


def fill_padded(pad, conv_ref, prior_ref):
    pad[0:8, :] = prior_ref[...].astype(F32)[8:16]
    pad[8:, :] = conv_ref[...].astype(F32)


def running_decay(decay_ref):
    rows = decay_ref.shape[1]
    lower = jnp.where(iota((rows, rows), 0) >= iota((rows, rows), 1), 1.0, 0.0)
    by_token = jnp.dot(lower, decay_ref[...].T, precision=HIGH, preferred_element_type=F32)
    return by_token


def front_part(
    far, finish_edges, conv_ref, prior_ref, w_ref, decay_ref, lw_ref, g_ref, totals_ref,
    u_ref, slope_ref, end_ref, gf_ref, fac_ref, pad, facs,
):
    me = lax.axis_index("ctx")
    rows, channels = g_ref.shape
    heads = decay_ref.shape[0]
    taps = w_ref.shape[0]
    pad[0:8, :] = jnp.zeros((8, pad.shape[1]), F32)
    pad[8:, :] = conv_ref[...].astype(F32)

    def activate(cols, count):
        top = 8 - taps + 1
        acc = w_ref[0:1, cols] * pad[top : top + count, cols]
        for k in range(1, taps):
            acc = acc + w_ref[k : k + 1, cols] * pad[top + k : top + k + count, cols]
        sig = jax.nn.sigmoid(acc)
        u_ref[0:count, cols] = (acc * sig).astype(BF16)
        slope_ref[0:count, cols] = sig * (1.0 + acc * (1.0 - sig))

    @pl.loop(0, pad.shape[1] // LANES)
    def _(j):
        activate(pl.ds(pl.multiple_of(j * LANES, LANES), LANES), rows)

    cum = running_decay(decay_ref)
    finish_edges()
    pad[0:8, :] = prior_ref[...].astype(F32)[8:16]

    @pl.loop(0, pad.shape[1] // LANES)
    def _(j):
        activate(pl.ds(pl.multiple_of(j * LANES, LANES), LANES), 16)

    totals = totals_ref[...][:, 0, :heads]
    spans = iota(totals.shape, 0)

    def span(lo, hi):
        return jnp.sum(jnp.where((spans >= lo) & (spans < hi), totals, 0.0), axis=0, keepdims=True)

    own, pre = [], []
    for level in range(far):
        half = me >> level
        upper = (half & 1) == 1
        start = half << level
        sib = (half ^ 1) << level
        size = 1 << level
        own.append(jnp.exp(jnp.where(upper, 0.0, 1.0) * span(sib, sib + size)))
        own.append(jnp.exp(jnp.where(upper, 1.0, 0.0) * span(start, start + size)))
        pre.append(jnp.where(upper, 1.0, 0.0) * jnp.exp(span(start, me)))
    count = fac_ref.shape[1]
    stack = own + pre
    if count > len(stack):
        stack.append(jnp.zeros((count - len(stack), heads), F32))
    small = jnp.concatenate(split2(jnp.concatenate(stack, axis=0)), axis=1)

    in_device = jnp.exp(cum)
    base = [jnp.exp(cum[rows - 1 : rows] - cum)]
    for level in range(far):
        base.append(in_device * lw_ref[2 + level].T * (level_scale(2 + level) * pre[level]))
    for idx, value in enumerate(base):
        facs[idx * rows : (idx + 1) * rows, :] = jnp.concatenate(split2(value), axis=1)

    bq = u_ref[:, channels:].astype(F32).T.astype(BF16)
    b_t = jnp.concatenate([bq[:BLOCK]] * 2, axis=1)
    q_t = jnp.concatenate([bq[BLOCK:]] * 2, axis=1)
    per_half = channels // 2 // LANES

    @pl.loop(0, channels // LANES)
    def _(j):
        cols = pl.ds(pl.multiple_of(j * LANES, LANES), LANES)
        side = j // per_half
        out = pl.ds(pl.multiple_of((j % per_half) * LANES, LANES), LANES)
        x = u_ref[:, cols].astype(F32)
        hot = one_hot(2 * heads, heads, 2 * j, LANES, BLOCK)
        spread = dot(facs[...], hot)
        fac_ref[side, :, out] = dot(small, hot)
        end_ref[side, :, out] = dot(b_t, jnp.concatenate(split2(x * spread[:rows]), axis=0))
        g = g_ref[:, cols].astype(F32)
        for level in range(far):
            inner = g * spread[(1 + level) * rows : (2 + level) * rows]
            gf_ref[level, side, :, out] = dot(q_t, jnp.concatenate(split2(inner), axis=0))


def near_setup(decay_ref, lw_ref, u_ref, glev_ref, facs, cum3, cum_rows, bias, scores, hotx, hotg, ds_acc):
    rows = decay_ref.shape[1]
    wide = 2 * rows
    cum = running_decay(decay_ref)
    cum_rows[...] = cum.T
    cum3[...] = jnp.concatenate(split3(cum), axis=1)
    for level in range(2):
        value = lw_ref[level].T * level_scale(level)
        facs[level * rows : (level + 1) * rows, :] = jnp.concatenate(split2(value), axis=1)
    first = iota((rows, wide), 0)
    second = iota((rows, wide), 1) % rows
    bias[0] = jnp.where(second <= first, 0.0, -1e30)
    bias[1] = jnp.where(first <= second, 0.0, -1e30)
    r, c = iota((wide, wide), 0), iota((wide, wide), 1)
    same = (r // rows) == (c % LANES) // BLOCK
    block1 = (r % rows) // BLOCK == 1
    hotg[...] = jnp.where(same, 1.0, 0.0).astype(BF16)
    hotx[...] = jnp.where(same & (block1 == (c < LANES)), 1.0, 0.0).astype(BF16)
    bq = u_ref[:, u_ref.shape[1] - LANES :]
    b, q = bq[:, :BLOCK], bq[:, BLOCK:]
    scores[0] = dot_nt(q, jnp.concatenate([b, b], axis=0))
    scores[1] = dot_nt(b, jnp.concatenate([q, q], axis=0))
    ds_acc[...] = jnp.zeros_like(ds_acc)
    glev_ref[...] = jnp.zeros_like(glev_ref)


def head_pick(heads, j):
    lanes = iota((heads, 2 * LANES), 1) % LANES
    return jnp.where(iota((heads, 2 * LANES), 0) == 2 * j + lanes // BLOCK, 1.0, 0.0).astype(BF16)


def near_pair(j, g_ref, u_ref, mixed_ref, dx_ref, glev_ref, facs, cum3, cum_rows, bias, scores, hotx, hotg, ds_acc):
    heads, rows = cum_rows.shape
    wide = 2 * rows
    low = iota((rows, LANES), 0) < BLOCK
    cols = pl.ds(pl.multiple_of(j * LANES, LANES), LANES)
    x = u_ref[:, cols]
    g = g_ref[:, cols].astype(F32)
    spread = dot(facs[...], one_hot(2 * heads, heads, 2 * j, LANES, BLOCK))
    w0, w1 = spread[:rows], spread[rows:]
    col = dot(cum3[...], one_hot(3 * heads, heads, 2 * j, wide, rows))
    row = jnp.concatenate([cum_rows[pl.ds(2 * j, 1), :], cum_rows[pl.ds(2 * j + 1, 1), :]], axis=1)
    gap = col - row
    decay = jnp.exp(gap + bias[0])
    mix = (scores[0] * decay).astype(BF16)
    mix_t = (scores[1] * jnp.exp(bias[1] - gap)).astype(BF16)
    wx = jnp.concatenate([jnp.concatenate([x, x], axis=1)] * 2, axis=0) * hotx[...]
    res = dot(mix, wx)
    out0 = jnp.where(low, res[:, LANES:], res[:, :LANES])
    out1 = jnp.where(low, 0.0, res[:, LANES:])
    gz = (g * w0).astype(BF16)
    gh = (g * jnp.where(low, w0, w1)).astype(BF16)
    gg = jnp.concatenate([gz, gh], axis=1)
    ds_acc[...] += decay * dot_nt(gg, wx)
    res = dot(mix_t, jnp.concatenate([gg, gg], axis=0) * hotg[...])
    dx_ref[:, cols] = jnp.where(low, res[:, LANES:], res[:, :LANES])
    mixed_ref[:, cols] = w0 * out0 + w1 * out1
    pick = head_pick(heads, j)
    for level, out in enumerate((out0, out1)):
        glev_ref[level] += dot_nt(pick, jnp.concatenate(split2(g * out), axis=1)) * level_scale(level)


def fenwick_part(
    far, end_ref, gf_ref, fac_ref, decay_ref, lw_ref, g_ref, u_ref,
    far_ref, grad_ref, mixed_ref, dx_ref, glev_ref, dbq_ref,
    facs, cum3, cum_rows, bias, scores, hotx, hotg, ds_acc,
    up0, up0_in, up, up_in, cross_in, merge, merge_in, down, down_in, last, last_in,
    sems_s, sems_r, run, back,
):
    me = lax.axis_index("ctx")
    core = me & 1
    other = 1 - core
    peers = [at(me ^ (1 << level)) for level in range(far)]

    def copy(src, dst, kind, level, peer):
        made = pltpu.make_async_remote_copy(
            src, dst, sems_s.at[kind, level], sems_r.at[kind, level], peer, MESH
        )
        made.start()
        return made

    pending = []
    up0[...] = end_ref[...].astype(BF16)
    for level in range(1, far):
        merge[level - 1] = gf_ref[level, other].astype(BF16)
    merge_copy = copy(merge, merge_in, 0, 0, peers[0])
    up_copy = copy(up0, up0_in, 1, 0, peers[0])
    crosses = []

    def own_coef(level):
        return fac_ref[core, 2 * level : 2 * level + 1, :]

    def sib_coef(level):
        return fac_ref[core, 2 * level + 1 : 2 * level + 2, :]

    near_setup(decay_ref, lw_ref, u_ref, glev_ref, facs, cum3, cum_rows, bias, scores, hotx, hotg, ds_acc)
    pairs = g_ref.shape[1] // LANES
    cuts = [0, 1] + [1 + (pairs - 1) * (step + 1) // (far - 1) for step in range(far - 1)]

    def near_part(lo, hi):
        @pl.loop(lo, hi)
        def _(j):
            near_pair(
                j, g_ref, u_ref, mixed_ref, dx_ref, glev_ref, facs, cum3, cum_rows, bias, scores, hotx, hotg, ds_acc
            )

    near_part(cuts[0], cuts[1])
    merge_copy.wait()
    pending_down = None
    for step in range(far - 1):
        level = far - 1 - step
        total = gf_ref[level, core] + merge_in[level - 1].astype(F32)
        if step > 0:
            pending_down.wait()
            back[...] = back[...] * own_coef(level + 1) if step > 1 else jnp.zeros_like(back)
            back[...] = back[...] + down_in[level].astype(F32)
            total = total + back[...] * sib_coef(level)
        down[level - 1] = total.astype(BF16)
        pending_down = copy(down.at[level - 1], down_in.at[level - 1], 2, level, peers[level])

        up_copy.wait()
        if step == 0:
            run[...] = end_ref[core] * own_coef(0) + up0_in[core].astype(F32) * sib_coef(0)
        else:
            crosses.append(copy(up_in.at[step - 1], cross_in.at[step - 1], 3, step, peers[0]))
            run[...] = run[...] * own_coef(step) + up_in[step - 1].astype(F32) * sib_coef(step)
        up[step] = run[...].astype(BF16)
        up_copy = copy(up.at[step], up_in.at[step], 1, step + 1, peers[step + 1])
        near_part(cuts[step + 1], cuts[step + 2])
    pending_down.wait()
    if far > 2:
        back[...] = back[...] * own_coef(1) + down_in[0].astype(F32)
    else:
        back[...] = down_in[0].astype(F32)
    last[core] = (gf_ref[0, core] + back[...] * sib_coef(0)).astype(BF16)
    last[other] = gf_ref[0, other].astype(BF16)
    last_copy = copy(last, last_in, 4, 0, peers[0])
    rows = decay_ref.shape[1]
    bq = u_ref[:, u_ref.shape[1] - LANES :]
    ds = ds_acc[:, :rows] + ds_acc[:, rows:]
    dq = dot(ds.astype(BF16), bq[:, :BLOCK])
    db = dot(ds.T.astype(BF16), bq[:, BLOCK:])
    dbq_ref[...] = jnp.concatenate([db, dq], axis=1)
    up_copy.wait()
    crosses.append(copy(up_in.at[far - 2], cross_in.at[far - 2], 3, far - 1, peers[0]))
    far_ref[0] = up0_in[...]
    for level in range(1, far):
        far_ref[level, core] = up_in[level - 1]
    last_copy.wait()
    grad_ref[core] = back[...] * own_coef(0) + last_in[core].astype(F32)
    grad_ref[other] = last_in[other].astype(F32)
    for level in range(1, far):
        crosses[level - 1].wait()
        far_ref[level, other] = cross_in[level - 1]


def travel_kernel(
    n, far, conv_ref, w_ref, decay_ref, lw_ref, g_ref,
    prior_ref, u_ref, slope_ref, fac_ref, far_ref, grad_ref, mixed_ref, dx_ref, glev_ref, dbq_ref,
    totals, mine, slots, rows, send, recv, rsend, rrecv, pad, facs, end, gf, *rest,
):
    finish = start_edges(n, conv_ref, decay_ref, prior_ref, totals, mine, slots, rows, send, recv, rsend, rrecv)
    front_part(
        far, finish, conv_ref, prior_ref, w_ref, decay_ref, lw_ref, g_ref, totals,
        u_ref, slope_ref, end, gf, fac_ref, pad, facs,
    )
    fenwick_part(
        far, end, gf, fac_ref, decay_ref, lw_ref, g_ref, u_ref,
        far_ref, grad_ref, mixed_ref, dx_ref, glev_ref, dbq_ref, *rest,
    )


def travel(n, conv_input, conv_weight, log_decay, level_weight, grad_out):
    far = n.bit_length() - 1
    heads, rows = log_decay.shape
    channels = grad_out.shape[1]
    conv_ch = conv_input.shape[1]
    piece = (BLOCK, channels // 2)
    half = (2,) + piece
    stack = (far - 1,) + piece
    fac_rows = (3 * far + 7) // 8 * 8
    shape = jax.ShapeDtypeStruct
    vm = pl.BlockSpec(memory_space=pltpu.VMEM)
    return pl.pallas_call(
        functools.partial(travel_kernel, n, far),
        out_shape=(
            shape((16, conv_ch), BF16),
            shape((rows, conv_ch), BF16),
            shape((rows, conv_ch), F32),
            shape((2, fac_rows, channels // 2), F32),
            shape((far,) + half, BF16),
            shape(half, F32),
            shape((rows, channels), F32),
            shape((rows, channels), F32),
            shape((2, heads, rows), F32),
            shape((rows, LANES), F32),
        ),
        in_specs=[vm] * 5,
        out_specs=(vm,) * 10,
        scratch_shapes=[
            pltpu.VMEM((n, 8, LANES), F32),
            pltpu.VMEM((8, LANES), F32),
            pltpu.VMEM((n - 1, 8, LANES), F32),
            pltpu.VMEM((16, conv_ch), BF16),
            pltpu.SemaphoreType.DMA((n - 1,)),
            pltpu.SemaphoreType.DMA((n - 1,)),
            pltpu.SemaphoreType.DMA,
            pltpu.SemaphoreType.DMA,
            pltpu.VMEM((rows + 8, conv_ch), F32),
            pltpu.VMEM(((1 + far) * rows, 2 * heads), BF16),
            pltpu.VMEM(half, F32),
            pltpu.VMEM((far,) + half, F32),
            pltpu.VMEM((2 * rows, 2 * heads), BF16),
            pltpu.VMEM((rows, 3 * heads), BF16),
            pltpu.VMEM((heads, rows), F32),
            pltpu.VMEM((2, rows, 2 * rows), F32),
            pltpu.VMEM((2, rows, 2 * rows), F32),
            pltpu.VMEM((2 * rows, 2 * rows), BF16),
            pltpu.VMEM((2 * rows, 2 * rows), BF16),
            pltpu.VMEM((rows, 2 * rows), F32),
            pltpu.VMEM(half, BF16),
            pltpu.VMEM(half, BF16),
            *[pltpu.VMEM(stack, BF16)] * 7,
            pltpu.VMEM(half, BF16),
            pltpu.VMEM(half, BF16),
            pltpu.SemaphoreType.DMA((5, far)),
            pltpu.SemaphoreType.DMA((5, far)),
            pltpu.VMEM(piece, F32),
            pltpu.VMEM(piece, F32),
        ],
        compiler_params=pltpu.CompilerParams(
            collective_id=0, has_side_effects=True, vmem_limit_bytes=VMEM_LIMIT
        ),
    )(conv_input, conv_weight, log_decay, level_weight, grad_out)


def back_kernel(
    far, conv_ref, prior_ref, w_ref, decay_ref, lw_ref, g_ref, u_ref, slope_ref, fac_ref, far_ref, grad_ref,
    near_ref, dx_ref, nlev_ref, dbq_ref,
    mixed_ref, gin_ref, glev_ref, tail_ref, head_ref, wpart_ref,
    pad, gp, facs, q_s, b2_s, dq_acc, db_acc,
):
    rows, channels = g_ref.shape
    heads = decay_ref.shape[0]
    taps = w_ref.shape[0]
    fill_padded(pad, conv_ref, prior_ref)
    cum = running_decay(decay_ref)
    base = [jnp.exp(cum[rows - 1 : rows] - cum), jnp.exp(cum)]
    base += [lw_ref[2 + level].T * level_scale(2 + level) for level in range(far)]
    for idx, value in enumerate(base):
        facs[idx * rows : (idx + 1) * rows, :] = jnp.concatenate(split2(value), axis=1)
    bq = u_ref[:, channels:]
    q_s[...] = bq[:, BLOCK:]
    b2_s[...] = jnp.concatenate([bq[:, :BLOCK]] * 2, axis=1)
    dq_acc[...] = jnp.zeros_like(dq_acc)
    db_acc[...] = jnp.zeros_like(db_acc)
    glev_ref[...] = jnp.zeros_like(glev_ref)
    glev_ref[0:2] = nlev_ref[...]
    per_half = channels // 2 // LANES

    @pl.loop(0, channels // LANES)
    def _(j):
        cols = pl.ds(pl.multiple_of(j * LANES, LANES), LANES)
        side = j // per_half
        part = pl.ds(pl.multiple_of((j % per_half) * LANES, LANES), LANES)
        x = u_ref[:, cols]
        g = g_ref[:, cols].astype(F32)
        spread = dot(facs[...], one_hot(2 * heads, heads, 2 * j, LANES, BLOCK))

        def fac(idx):
            return spread[idx * rows : (idx + 1) * rows]

        mixed = near_ref[:, cols]
        products, inner, states = [], [], []
        for level in range(far):
            state = far_ref[level, side, :, part]
            scale = fac(1) * fac_ref[side, 2 * far + level : 2 * far + level + 1, part]
            out = dot(q_s[...], state) * scale
            weight = fac(2 + level)
            mixed = mixed + weight * out
            products.append(g * out)
            inner.append((g * weight * scale).astype(BF16))
            states.append(state)
        mixed_ref[:, cols] = mixed.astype(BF16)
        dq_acc[...] += dot_nt(jnp.concatenate(inner, axis=1), jnp.concatenate(states, axis=1))
        pick = head_pick(heads, j)
        for level, product in enumerate(products):
            sums = dot_nt(pick, jnp.concatenate(split2(product), axis=1))
            glev_ref[2 + level] += sums * level_scale(2 + level)

        grad = grad_ref[side, :, part]
        hi, lo = split2(grad)
        key_decay = fac(0)
        dx = dx_ref[:, cols] + key_decay * dot(b2_s[...], jnp.concatenate([hi, lo], axis=0))
        db_acc[...] += dot_nt((x.astype(F32) * key_decay).astype(BF16), hi)
        gp[0:rows, cols] = dx * slope_ref[:, cols]

    dbq = dbq_ref[...] + jnp.concatenate([db_acc[...], dq_acc[...]], axis=1)
    gp[0:rows, channels:] = dbq * slope_ref[:, channels:]
    gp[rows:, :] = jnp.zeros((8, gp.shape[1]), F32)
    head_ref[...] = gp[0:8, :]

    @pl.loop(0, gp.shape[1] // LANES)
    def _(j):
        cols = pl.ds(pl.multiple_of(j * LANES, LANES), LANES)
        grad = gp[0:rows, cols]
        acc = w_ref[taps - 1 : taps, cols] * grad
        sums = []
        for k in range(taps):
            shift = taps - 1 - k
            if shift:
                acc = acc + w_ref[k : k + 1, cols] * gp[shift : shift + rows, cols]
            sums.append(jnp.sum(pad[8 - shift : 8 - shift + rows, cols] * grad, axis=0, keepdims=True))
        gin_ref[:, cols] = acc.astype(BF16)
        tail_ref[:, cols] = acc[rows - 16 :]
        sums.append(jnp.zeros((8 - taps, LANES), F32))
        wpart_ref[:, cols] = jnp.concatenate(sums, axis=0)


def finish_kernel(n, digits, tail_ref, head_ref, wpart_ref, w_ref, out_ref, wsum_ref, lead, nxt, acc, slots, hs, hr, send, recv):
    me = lax.axis_index("ctx")
    taps = w_ref.shape[0]
    channels = w_ref.shape[1]
    width = acc.shape[2]
    skip = channels - width

    def packed(rows):
        return jnp.concatenate([rows[:4, :width], rows[:4, skip:]], axis=0)

    def unpacked(value):
        return jnp.concatenate([value[:4, :skip], value[4:]], axis=1)

    lead[...] = packed(head_ref[...])
    acc[0] = packed(wpart_ref[...])
    before, after = lax.rem(me + n - 1, n), lax.rem(me + 1, n)
    plan = []
    for shift, size in digits:
        digit = (me >> shift) & (size - 1)
        plan.append((digit, [me ^ (d << shift) for d in range(1, size)]))
    greet([at(before), at(after)] + [at(p) for _, peers in plan for p in peers])
    row_copy = pltpu.make_async_remote_copy(lead, nxt, hs, hr, at(before), MESH)
    row_copy.start()
    for stage, (digit, peers) in enumerate(plan):
        copies = []
        for d, peer in enumerate(peers):
            copy = pltpu.make_async_remote_copy(
                acc.at[stage], slots.at[stage, d], send.at[stage, d], recv.at[stage, d], at(peer), MESH
            )
            copy.start()
            copies.append(copy)
        if stage == 0:
            row_copy.wait()
            keep = jnp.where(me < n - 1, 1.0, 0.0)
            rows = unpacked(nxt[...]) * keep
            blank = jnp.zeros((8, channels), F32)
            joined = jnp.concatenate([blank, rows, blank[:4]], axis=0)
            fix = blank
            for k in range(taps - 1):
                shift = taps - 1 - k
                fix = fix + w_ref[k : k + 1, :] * joined[shift : shift + 8]
            out_ref[...] = (tail_ref[...] + jnp.concatenate([jnp.zeros_like(fix), fix], axis=0)).astype(BF16)
        for copy in copies:
            copy.wait()
        size = len(peers) + 1
        have = [acc[stage]] + [slots[stage, d] for d in range(size - 1)]
        if size == 2:
            total = have[0] + have[1]
        else:
            total = (have[0] + have[1]) + (have[2] + have[3])
        acc[stage + 1] = total
    wsum_ref[...] = unpacked(acc[len(plan)])[:taps]


def exchange_finish(n, tail, head, wpart, conv_weight):
    far = n.bit_length() - 1
    digits = []
    shift = 0
    while shift < far:
        bits = min(2, far - shift)
        digits.append((shift, 1 << bits))
        shift += bits
    channels = tail.shape[1]
    width = (channels // LANES + 1) // 2 * LANES
    vm = pl.BlockSpec(memory_space=pltpu.VMEM)
    return pl.pallas_call(
        functools.partial(finish_kernel, n, digits),
        out_shape=(
            jax.ShapeDtypeStruct((16, channels), BF16),
            jax.ShapeDtypeStruct(conv_weight.shape, F32),
        ),
        in_specs=[vm] * 4,
        out_specs=(vm, vm),
        scratch_shapes=[
            pltpu.VMEM((8, width), F32),
            pltpu.VMEM((8, width), F32),
            pltpu.VMEM((len(digits) + 1, 8, width), F32),
            pltpu.VMEM((len(digits), 3, 8, width), F32),
            pltpu.SemaphoreType.DMA,
            pltpu.SemaphoreType.DMA,
            pltpu.SemaphoreType.DMA((len(digits), 3)),
            pltpu.SemaphoreType.DMA((len(digits), 3)),
        ],
        compiler_params=pltpu.CompilerParams(
            collective_id=2, has_side_effects=True, vmem_limit_bytes=VMEM_LIMIT
        ),
    )(tail, head, wpart, conv_weight)


def body(conv_input, conv_weight, log_decay, level_weight, grad_out):
    n = lax.axis_size("ctx")
    far = n.bit_length() - 1
    rows, conv_ch = conv_input.shape
    channels = grad_out.shape[1]
    heads = log_decay.shape[0]
    vm = pl.BlockSpec(memory_space=pltpu.VMEM)
    params = pltpu.CompilerParams(vmem_limit_bytes=VMEM_LIMIT)
    shape = jax.ShapeDtypeStruct
    prior, u_act, slope, factors, far_states, grad_end, *near = travel(
        n, conv_input, conv_weight, log_decay, level_weight, grad_out
    )
    mixed, grad_input, grad_level, tail, head, wpart = pl.pallas_call(
        functools.partial(back_kernel, far),
        out_shape=(
            shape((rows, channels), BF16),
            shape((rows, conv_ch), BF16),
            shape(level_weight.shape, F32),
            shape((16, conv_ch), F32),
            shape((8, conv_ch), F32),
            shape((8, conv_ch), F32),
        ),
        in_specs=[vm] * 15,
        out_specs=(vm,) * 6,
        scratch_shapes=[
            pltpu.VMEM((rows + 8, conv_ch), F32),
            pltpu.VMEM((rows + 8, conv_ch), F32),
            pltpu.VMEM(((2 + far) * rows, 2 * heads), BF16),
            pltpu.VMEM((rows, BLOCK), BF16),
            pltpu.VMEM((rows, 2 * BLOCK), BF16),
            pltpu.VMEM((rows, BLOCK), F32),
            pltpu.VMEM((rows, BLOCK), F32),
        ],
        compiler_params=params,
    )(
        conv_input, prior, conv_weight, log_decay, level_weight, grad_out,
        u_act, slope, factors, far_states, grad_end, *near,
    )
    tail_rows, weight_grad = exchange_finish(n, tail, head, wpart, conv_weight)
    grad_input = lax.dynamic_update_slice(grad_input, tail_rows, (rows - 16, 0))
    return (mixed, grad_input, grad_level, weight_grad)


def solution(mesh):
    in_specs = (
        P(("groups", "ctx"), None),
        P(),
        P(None, ("groups", "ctx")),
        P(None, None, ("groups", "ctx")),
        P(("groups", "ctx"), None),
    )
    out_specs = (
        P(("groups", "ctx"), None),
        P(("groups", "ctx"), None),
        P(None, None, ("groups", "ctx")),
        P("groups", None),
    )
    return jax.shard_map(body, mesh=mesh, in_specs=in_specs, out_specs=out_specs, check_vma=False)
```

```python
import functools

import jax
import jax.numpy as jnp
from jax import lax
from jax.experimental import pallas as pl
from jax.experimental.pallas import tpu as pltpu
from jax.sharding import PartitionSpec as P

BLOCK = 64
LANES = 128
MESH = pl.DeviceIdType.MESH
HIGH = lax.Precision.HIGHEST
F32 = jnp.float32
BF16 = jnp.bfloat16
VMEM_LIMIT = 56 * 1024 * 1024


def level_scale(level_idx):
    if level_idx == 0:
        return BLOCK**-0.5
    return (BLOCK * 2 ** (level_idx - 1)) ** -0.5


def dot(a, b):
    return jnp.dot(a, b, preferred_element_type=F32)


def dot_nt(a, b):
    return lax.dot_general(a, b, (((1,), (1,)), ((), ())), preferred_element_type=F32)


def split2(v):
    hi = v.astype(BF16)
    return hi, (v - hi.astype(F32)).astype(BF16)


def split3(v):
    hi = v.astype(BF16)
    rest = v - hi.astype(F32)
    mid = rest.astype(BF16)
    return hi, mid, (rest - mid.astype(F32)).astype(BF16)


def iota(shape, axis):
    return lax.broadcasted_iota(jnp.int32, shape, axis)


def one_hot(rows, heads, first, lanes, width):
    return jnp.where(
        iota((rows, lanes), 0) % heads == first + iota((rows, lanes), 1) // width, 1.0, 0.0
    ).astype(BF16)


def greet(peers):
    barrier = pltpu.get_barrier_semaphore()
    for peer in peers:
        pl.semaphore_signal(barrier, inc=1, device_id=peer, device_id_type=MESH)
    pl.semaphore_wait(barrier, len(peers))


def at(peer):
    return (lax.axis_index("groups"), peer)


def start_edges(n, conv_ref, decay_ref, prior_ref, totals_ref, mine, slots, rows, send, recv, rsend, rrecv):
    me = lax.axis_index("ctx")
    peers = [lax.rem(me + d, n) for d in range(1, n)]
    heads = decay_ref.shape[0]
    mine[...] = jnp.zeros_like(mine)
    mine[:, :heads] = lax.dot_general(
        jnp.ones((8, decay_ref.shape[1]), F32),
        decay_ref[...],
        (((1,), (1,)), ((), ())),
        precision=HIGH,
        preferred_element_type=F32,
    )
    greet([at(p) for p in peers])
    copies = []
    count = conv_ref.shape[0]
    row_copy = pltpu.make_async_remote_copy(
        conv_ref.at[pl.ds(count - 16, 16), :], rows, rsend, rrecv, at(peers[0]), MESH
    )
    row_copy.start()
    for d in range(1, n):
        copy = pltpu.make_async_remote_copy(
            mine, slots.at[d - 1], send.at[d - 1], recv.at[d - 1], at(peers[d - 1]), MESH
        )
        copy.start()
        copies.append(copy)
    totals_ref[me] = mine[...]

    def finish():
        for d in range(1, n):
            copies[d - 1].wait()
            totals_ref[lax.rem(me - d + n, n)] = slots[d - 1]
        row_copy.wait()
        keep = jnp.where(me > 0, 1.0, 0.0)
        prior_ref[...] = (rows[...].astype(F32) * keep).astype(BF16)

    return finish


def fill_padded(pad, conv_ref, prior_ref):
    pad[0:8, :] = prior_ref[...].astype(F32)[8:16]
    pad[8:, :] = conv_ref[...].astype(F32)


def running_decay(decay_ref):
    rows = decay_ref.shape[1]
    lower = jnp.where(iota((rows, rows), 0) >= iota((rows, rows), 1), 1.0, 0.0)
    by_token = jnp.dot(lower, decay_ref[...].T, precision=HIGH, preferred_element_type=F32)
    return by_token


def front_part(
    far, finish_edges, conv_ref, prior_ref, w_ref, decay_ref, lw_ref, g_ref, totals_ref,
    u_ref, slope_ref, end_ref, gf_ref, fac_ref, pad, facs,
):
    me = lax.axis_index("ctx")
    rows, channels = g_ref.shape
    heads = decay_ref.shape[0]
    taps = w_ref.shape[0]
    pad[0:8, :] = jnp.zeros((8, pad.shape[1]), F32)
    pad[8:, :] = conv_ref[...].astype(F32)

    def activate(cols, count):
        top = 8 - taps + 1
        acc = w_ref[0:1, cols] * pad[top : top + count, cols]
        for k in range(1, taps):
            acc = acc + w_ref[k : k + 1, cols] * pad[top + k : top + k + count, cols]
        sig = jax.nn.sigmoid(acc)
        u_ref[0:count, cols] = (acc * sig).astype(BF16)
        slope_ref[0:count, cols] = sig * (1.0 + acc * (1.0 - sig))

    @pl.loop(0, pad.shape[1] // LANES)
    def _(j):
        activate(pl.ds(pl.multiple_of(j * LANES, LANES), LANES), rows)

    cum = running_decay(decay_ref)
    finish_edges()
    pad[0:8, :] = prior_ref[...].astype(F32)[8:16]

    @pl.loop(0, pad.shape[1] // LANES)
    def _(j):
        activate(pl.ds(pl.multiple_of(j * LANES, LANES), LANES), 16)

    totals = totals_ref[...][:, 0, :heads]
    spans = iota(totals.shape, 0)

    def span(lo, hi):
        return jnp.sum(jnp.where((spans >= lo) & (spans < hi), totals, 0.0), axis=0, keepdims=True)

    own, pre = [], []
    for level in range(far):
        half = me >> level
        upper = (half & 1) == 1
        start = half << level
        sib = (half ^ 1) << level
        size = 1 << level
        own.append(jnp.exp(jnp.where(upper, 0.0, 1.0) * span(sib, sib + size)))
        own.append(jnp.exp(jnp.where(upper, 1.0, 0.0) * span(start, start + size)))
        pre.append(jnp.where(upper, 1.0, 0.0) * jnp.exp(span(start, me)))
    count = fac_ref.shape[1]
    stack = own + pre
    if count > len(stack):
        stack.append(jnp.zeros((count - len(stack), heads), F32))
    small = jnp.concatenate(split2(jnp.concatenate(stack, axis=0)), axis=1)

    in_device = jnp.exp(cum)
    base = [jnp.exp(cum[rows - 1 : rows] - cum)]
    for level in range(far):
        base.append(in_device * lw_ref[2 + level].T * (level_scale(2 + level) * pre[level]))
    for idx, value in enumerate(base):
        facs[idx * rows : (idx + 1) * rows, :] = jnp.concatenate(split2(value), axis=1)

    bq = u_ref[:, channels:].astype(F32).T.astype(BF16)
    b_t = jnp.concatenate([bq[:BLOCK]] * 2, axis=1)
    q_t = jnp.concatenate([bq[BLOCK:]] * 2, axis=1)
    per_half = channels // 2 // LANES

    @pl.loop(0, channels // LANES)
    def _(j):
        cols = pl.ds(pl.multiple_of(j * LANES, LANES), LANES)
        side = j // per_half
        out = pl.ds(pl.multiple_of((j % per_half) * LANES, LANES), LANES)
        x = u_ref[:, cols].astype(F32)
        hot = one_hot(2 * heads, heads, 2 * j, LANES, BLOCK)
        spread = dot(facs[...], hot)
        fac_ref[side, :, out] = dot(small, hot)
        end_ref[side, :, out] = dot(b_t, jnp.concatenate(split2(x * spread[:rows]), axis=0))
        g = g_ref[:, cols].astype(F32)
        for level in range(far):
            inner = g * spread[(1 + level) * rows : (2 + level) * rows]
            gf_ref[level, side, :, out] = dot(q_t, jnp.concatenate(split2(inner), axis=0))


def near_setup(decay_ref, lw_ref, u_ref, glev_ref, facs, cum3, cum_rows, bias, scores, hotx, hotg, ds_acc):
    rows = decay_ref.shape[1]
    wide = 2 * rows
    cum = running_decay(decay_ref)
    cum_rows[...] = cum.T
    cum3[...] = jnp.concatenate(split3(cum), axis=1)
    for level in range(2):
        value = lw_ref[level].T * level_scale(level)
        facs[level * rows : (level + 1) * rows, :] = jnp.concatenate(split2(value), axis=1)
    first = iota((rows, wide), 0)
    second = iota((rows, wide), 1) % rows
    bias[0] = jnp.where(second <= first, 0.0, -1e30)
    bias[1] = jnp.where(first <= second, 0.0, -1e30)
    r, c = iota((wide, wide), 0), iota((wide, wide), 1)
    same = (r // rows) == (c % LANES) // BLOCK
    block1 = (r % rows) // BLOCK == 1
    hotg[...] = jnp.where(same, 1.0, 0.0).astype(BF16)
    hotx[...] = jnp.where(same & (block1 == (c < LANES)), 1.0, 0.0).astype(BF16)
    bq = u_ref[:, u_ref.shape[1] - LANES :]
    b, q = bq[:, :BLOCK], bq[:, BLOCK:]
    scores[0] = dot_nt(q, jnp.concatenate([b, b], axis=0))
    scores[1] = dot_nt(b, jnp.concatenate([q, q], axis=0))
    ds_acc[...] = jnp.zeros_like(ds_acc)
    glev_ref[...] = jnp.zeros_like(glev_ref)


def head_pick(heads, j):
    lanes = iota((heads, 2 * LANES), 1) % LANES
    return jnp.where(iota((heads, 2 * LANES), 0) == 2 * j + lanes // BLOCK, 1.0, 0.0).astype(BF16)


def near_pair(j, g_ref, u_ref, mixed_ref, dx_ref, glev_ref, facs, cum3, cum_rows, bias, scores, hotx, hotg, ds_acc):
    heads, rows = cum_rows.shape
    wide = 2 * rows
    low = iota((rows, LANES), 0) < BLOCK
    cols = pl.ds(pl.multiple_of(j * LANES, LANES), LANES)
    x = u_ref[:, cols]
    g = g_ref[:, cols].astype(F32)
    spread = dot(facs[...], one_hot(2 * heads, heads, 2 * j, LANES, BLOCK))
    w0, w1 = spread[:rows], spread[rows:]
    col = dot(cum3[...], one_hot(3 * heads, heads, 2 * j, wide, rows))
    row = jnp.concatenate([cum_rows[pl.ds(2 * j, 1), :], cum_rows[pl.ds(2 * j + 1, 1), :]], axis=1)
    gap = col - row
    decay = jnp.exp(gap + bias[0])
    mix = (scores[0] * decay).astype(BF16)
    mix_t = (scores[1] * jnp.exp(bias[1] - gap)).astype(BF16)
    wx = jnp.concatenate([jnp.concatenate([x, x], axis=1)] * 2, axis=0) * hotx[...]
    res = dot(mix, wx)
    out0 = jnp.where(low, res[:, LANES:], res[:, :LANES])
    out1 = jnp.where(low, 0.0, res[:, LANES:])
    gz = (g * w0).astype(BF16)
    gh = (g * jnp.where(low, w0, w1)).astype(BF16)
    gg = jnp.concatenate([gz, gh], axis=1)
    ds_acc[...] += decay * dot_nt(gg, wx)
    res = dot(mix_t, jnp.concatenate([gg, gg], axis=0) * hotg[...])
    dx_ref[:, cols] = jnp.where(low, res[:, LANES:], res[:, :LANES])
    mixed_ref[:, cols] = w0 * out0 + w1 * out1
    pick = head_pick(heads, j)
    for level, out in enumerate((out0, out1)):
        glev_ref[level] += dot_nt(pick, jnp.concatenate(split2(g * out), axis=1)) * level_scale(level)


def fenwick_part(
    far, end_ref, gf_ref, fac_ref, decay_ref, lw_ref, g_ref, u_ref,
    far_ref, grad_ref, mixed_ref, dx_ref, glev_ref, dbq_ref,
    facs, cum3, cum_rows, bias, scores, hotx, hotg, ds_acc,
    up0, up0_in, up, up_in, cross_in, merge, merge_in, down, down_in, last, last_in,
    sems_s, sems_r, run, back,
):
    me = lax.axis_index("ctx")
    core = me & 1
    other = 1 - core
    peers = [at(me ^ (1 << level)) for level in range(far)]

    def copy(src, dst, kind, level, peer):
        made = pltpu.make_async_remote_copy(
            src, dst, sems_s.at[kind, level], sems_r.at[kind, level], peer, MESH
        )
        made.start()
        return made

    pending = []
    up0[...] = end_ref[...].astype(BF16)
    for level in range(1, far):
        merge[level - 1] = gf_ref[level, other].astype(BF16)
    merge_copy = copy(merge, merge_in, 0, 0, peers[0])
    up_copy = copy(up0, up0_in, 1, 0, peers[0])
    crosses = []

    def own_coef(level):
        return fac_ref[core, 2 * level : 2 * level + 1, :]

    def sib_coef(level):
        return fac_ref[core, 2 * level + 1 : 2 * level + 2, :]

    near_setup(decay_ref, lw_ref, u_ref, glev_ref, facs, cum3, cum_rows, bias, scores, hotx, hotg, ds_acc)
    pairs = g_ref.shape[1] // LANES
    cuts = [0, 1] + [1 + (pairs - 1) * (step + 1) // (far - 1) for step in range(far - 1)]

    def near_part(lo, hi):
        @pl.loop(lo, hi)
        def _(j):
            near_pair(
                j, g_ref, u_ref, mixed_ref, dx_ref, glev_ref, facs, cum3, cum_rows, bias, scores, hotx, hotg, ds_acc
            )

    near_part(cuts[0], cuts[1])
    merge_copy.wait()
    pending_down = None
    for step in range(far - 1):
        level = far - 1 - step
        total = gf_ref[level, core] + merge_in[level - 1].astype(F32)
        if step > 0:
            pending_down.wait()
            back[...] = back[...] * own_coef(level + 1) if step > 1 else jnp.zeros_like(back)
            back[...] = back[...] + down_in[level].astype(F32)
            total = total + back[...] * sib_coef(level)
        down[level - 1] = total.astype(BF16)
        pending_down = copy(down.at[level - 1], down_in.at[level - 1], 2, level, peers[level])

        up_copy.wait()
        if step == 0:
            run[...] = end_ref[core] * own_coef(0) + up0_in[core].astype(F32) * sib_coef(0)
        else:
            crosses.append(copy(up_in.at[step - 1], cross_in.at[step - 1], 3, step, peers[0]))
            run[...] = run[...] * own_coef(step) + up_in[step - 1].astype(F32) * sib_coef(step)
        up[step] = run[...].astype(BF16)
        up_copy = copy(up.at[step], up_in.at[step], 1, step + 1, peers[step + 1])
        near_part(cuts[step + 1], cuts[step + 2])
    pending_down.wait()
    if far > 2:
        back[...] = back[...] * own_coef(1) + down_in[0].astype(F32)
    else:
        back[...] = down_in[0].astype(F32)
    last[core] = (gf_ref[0, core] + back[...] * sib_coef(0)).astype(BF16)
    last[other] = gf_ref[0, other].astype(BF16)
    last_copy = copy(last, last_in, 4, 0, peers[0])
    rows = decay_ref.shape[1]
    bq = u_ref[:, u_ref.shape[1] - LANES :]
    ds = ds_acc[:, :rows] + ds_acc[:, rows:]
    dq = dot(ds.astype(BF16), bq[:, :BLOCK])
    db = dot(ds.T.astype(BF16), bq[:, BLOCK:])
    dbq_ref[...] = jnp.concatenate([db, dq], axis=1)
    up_copy.wait()
    crosses.append(copy(up_in.at[far - 2], cross_in.at[far - 2], 3, far - 1, peers[0]))
    far_ref[0] = up0_in[...]
    for level in range(1, far):
        far_ref[level, core] = up_in[level - 1]
    last_copy.wait()
    grad_ref[core] = back[...] * own_coef(0) + last_in[core].astype(F32)
    grad_ref[other] = last_in[other].astype(F32)
    for level in range(1, far):
        crosses[level - 1].wait()
        far_ref[level, other] = cross_in[level - 1]


def back_part(
    far, conv_ref, prior_ref, w_ref, decay_ref, lw_ref, g_ref, u_ref, slope_ref, fac_ref, far_ref, grad_ref,
    near_ref, dx_ref, nlev_ref, dbq_ref,
    mixed_ref, gin_ref, glev_ref, tail_ref, head_ref, wpart_ref,
    pad, gp, facs, q_s, b2_s, dq_acc, db_acc,
):
    rows, channels = g_ref.shape
    heads = decay_ref.shape[0]
    taps = w_ref.shape[0]
    fill_padded(pad, conv_ref, prior_ref)
    cum = running_decay(decay_ref)
    base = [jnp.exp(cum[rows - 1 : rows] - cum), jnp.exp(cum)]
    base += [lw_ref[2 + level].T * level_scale(2 + level) for level in range(far)]
    for idx, value in enumerate(base):
        facs[idx * rows : (idx + 1) * rows, :] = jnp.concatenate(split2(value), axis=1)
    bq = u_ref[:, channels:]
    q_s[...] = bq[:, BLOCK:]
    b2_s[...] = jnp.concatenate([bq[:, :BLOCK]] * 2, axis=1)
    dq_acc[...] = jnp.zeros_like(dq_acc)
    db_acc[...] = jnp.zeros_like(db_acc)
    glev_ref[...] = jnp.zeros_like(glev_ref)
    glev_ref[0:2] = nlev_ref[...]
    per_half = channels // 2 // LANES

    @pl.loop(0, channels // LANES)
    def _(j):
        cols = pl.ds(pl.multiple_of(j * LANES, LANES), LANES)
        side = j // per_half
        part = pl.ds(pl.multiple_of((j % per_half) * LANES, LANES), LANES)
        x = u_ref[:, cols]
        g = g_ref[:, cols].astype(F32)
        spread = dot(facs[...], one_hot(2 * heads, heads, 2 * j, LANES, BLOCK))

        def fac(idx):
            return spread[idx * rows : (idx + 1) * rows]

        mixed = near_ref[:, cols]
        products, inner, states = [], [], []
        for level in range(far):
            state = far_ref[level, side, :, part]
            scale = fac(1) * fac_ref[side, 2 * far + level : 2 * far + level + 1, part]
            out = dot(q_s[...], state) * scale
            weight = fac(2 + level)
            mixed = mixed + weight * out
            products.append(g * out)
            inner.append((g * weight * scale).astype(BF16))
            states.append(state)
        mixed_ref[:, cols] = mixed.astype(BF16)
        dq_acc[...] += dot_nt(jnp.concatenate(inner, axis=1), jnp.concatenate(states, axis=1))
        pick = head_pick(heads, j)
        for level, product in enumerate(products):
            sums = dot_nt(pick, jnp.concatenate(split2(product), axis=1))
            glev_ref[2 + level] += sums * level_scale(2 + level)

        grad = grad_ref[side, :, part]
        hi, lo = split2(grad)
        key_decay = fac(0)
        dx = dx_ref[:, cols] + key_decay * dot(b2_s[...], jnp.concatenate([hi, lo], axis=0))
        db_acc[...] += dot_nt((x.astype(F32) * key_decay).astype(BF16), hi)
        gp[0:rows, cols] = dx * slope_ref[:, cols]

    dbq = dbq_ref[...] + jnp.concatenate([db_acc[...], dq_acc[...]], axis=1)
    gp[0:rows, channels:] = dbq * slope_ref[:, channels:]
    gp[rows:, :] = jnp.zeros((8, gp.shape[1]), F32)
    head_ref[...] = gp[0:8, :]

    @pl.loop(0, gp.shape[1] // LANES)
    def _(j):
        cols = pl.ds(pl.multiple_of(j * LANES, LANES), LANES)
        grad = gp[0:rows, cols]
        acc = w_ref[taps - 1 : taps, cols] * grad
        sums = []
        for k in range(taps):
            shift = taps - 1 - k
            if shift:
                acc = acc + w_ref[k : k + 1, cols] * gp[shift : shift + rows, cols]
            sums.append(jnp.sum(pad[8 - shift : 8 - shift + rows, cols] * grad, axis=0, keepdims=True))
        gin_ref[:, cols] = acc.astype(BF16)
        tail_ref[:, cols] = acc[rows - 16 :]
        sums.append(jnp.zeros((8 - taps, LANES), F32))
        wpart_ref[:, cols] = jnp.concatenate(sums, axis=0)


def finish_part(digits, n, tail_ref, head_ref, wpart_ref, w_ref, gin_ref, wsum_ref, lead, nxt, acc, slots, hs, hr, send, recv):
    me = lax.axis_index("ctx")
    taps = w_ref.shape[0]
    channels = w_ref.shape[1]
    width = acc.shape[2]
    skip = channels - width

    def packed(rows):
        return jnp.concatenate([rows[:4, :width], rows[:4, skip:]], axis=0)

    def unpacked(value):
        return jnp.concatenate([value[:4, :skip], value[4:]], axis=1)

    lead[...] = packed(head_ref[...])
    acc[0] = packed(wpart_ref[...])
    before = lax.rem(me + n - 1, n)
    plan = []
    for shift, size in digits:
        digit = (me >> shift) & (size - 1)
        plan.append((digit, [me ^ (d << shift) for d in range(1, size)]))
    row_copy = pltpu.make_async_remote_copy(lead, nxt, hs, hr, at(before), MESH)
    row_copy.start()
    for stage, (digit, peers) in enumerate(plan):
        copies = []
        for d, peer in enumerate(peers):
            copy = pltpu.make_async_remote_copy(
                acc.at[stage], slots.at[stage, d], send.at[stage, d], recv.at[stage, d], at(peer), MESH
            )
            copy.start()
            copies.append(copy)
        if stage == 0:
            row_copy.wait()
            keep = jnp.where(me < n - 1, 1.0, 0.0)
            rows = unpacked(nxt[...]) * keep
            blank = jnp.zeros((8, channels), F32)
            joined = jnp.concatenate([blank, rows, blank[:4]], axis=0)
            fix = blank
            for k in range(taps - 1):
                shift = taps - 1 - k
                fix = fix + w_ref[k : k + 1, :] * joined[shift : shift + 8]
            gin_ref[gin_ref.shape[0] - 16 :, :] = (tail_ref[...] + jnp.concatenate([jnp.zeros_like(fix), fix], axis=0)).astype(BF16)
        for copy in copies:
            copy.wait()
        size = len(peers) + 1
        have = [acc[stage]] + [slots[stage, d] for d in range(size - 1)]
        if size == 2:
            total = have[0] + have[1]
        else:
            total = (have[0] + have[1]) + (have[2] + have[3])
        acc[stage + 1] = total
    wsum_ref[...] = unpacked(acc[len(plan)])[:taps]


def travel_kernel(
    n, far, digits, conv_ref, w_ref, decay_ref, lw_ref, g_ref,
    mixed_ref, gin_ref, glev_ref, wsum_ref,
    prior_ref, u_ref, slope_ref, fac_ref, far_ref, grad_ref, near_ref, dx_ref, nlev_ref, dbq_ref,
    tail, head, wpart, gp, bfacs, q_s, b2_s, dq_acc, db_acc, lead, nxt, acc, tslots, hs, hr, tsend, trecv,
    totals, mine, slots, rows, send, recv, rsend, rrecv, pad, facs, end, gf, *rest,
):
    finish = start_edges(n, conv_ref, decay_ref, prior_ref, totals, mine, slots, rows, send, recv, rsend, rrecv)
    front_part(
        far, finish, conv_ref, prior_ref, w_ref, decay_ref, lw_ref, g_ref, totals,
        u_ref, slope_ref, end, gf, fac_ref, pad, facs,
    )
    fenwick_part(
        far, end, gf, fac_ref, decay_ref, lw_ref, g_ref, u_ref,
        far_ref, grad_ref, near_ref, dx_ref, nlev_ref, dbq_ref, *rest,
    )
    back_part(
        far, conv_ref, prior_ref, w_ref, decay_ref, lw_ref, g_ref, u_ref, slope_ref, fac_ref, far_ref, grad_ref,
        near_ref, dx_ref, nlev_ref, dbq_ref,
        mixed_ref, gin_ref, glev_ref, tail, head, wpart,
        pad, gp, bfacs, q_s, b2_s, dq_acc, db_acc,
    )
    finish_part(digits, n, tail, head, wpart, w_ref, gin_ref, wsum_ref, lead, nxt, acc, tslots, hs, hr, tsend, trecv)


def travel(n, conv_input, conv_weight, log_decay, level_weight, grad_out):
    far = n.bit_length() - 1
    heads, rows = log_decay.shape
    channels = grad_out.shape[1]
    conv_ch = conv_input.shape[1]
    piece = (BLOCK, channels // 2)
    half = (2,) + piece
    stack = (far - 1,) + piece
    fac_rows = (3 * far + 7) // 8 * 8
    shape = jax.ShapeDtypeStruct
    digits = [(shift, 1 << min(2, far - shift)) for shift in range(0, far, 2)]
    width = (conv_ch // LANES + 1) // 2 * LANES
    vm = pl.BlockSpec(memory_space=pltpu.VMEM)
    return pl.pallas_call(
        functools.partial(travel_kernel, n, far, digits),
        out_shape=(
            shape((rows, channels), BF16),
            shape((rows, conv_ch), BF16),
            shape(level_weight.shape, F32),
            shape(conv_weight.shape, F32),
        ),
        in_specs=[vm] * 5,
        out_specs=(vm,) * 4,
        scratch_shapes=[
            pltpu.VMEM((16, conv_ch), BF16),
            pltpu.VMEM((rows, conv_ch), BF16),
            pltpu.VMEM((rows, conv_ch), F32),
            pltpu.VMEM((2, fac_rows, channels // 2), F32),
            pltpu.VMEM((far,) + half, BF16),
            pltpu.VMEM(half, F32),
            pltpu.VMEM((rows, channels), F32),
            pltpu.VMEM((rows, channels), F32),
            pltpu.VMEM((2, heads, rows), F32),
            pltpu.VMEM((rows, LANES), F32),
            pltpu.VMEM((16, conv_ch), F32),
            pltpu.VMEM((8, conv_ch), F32),
            pltpu.VMEM((8, conv_ch), F32),
            pltpu.VMEM((rows + 8, conv_ch), F32),
            pltpu.VMEM(((2 + far) * rows, 2 * heads), BF16),
            pltpu.VMEM((rows, BLOCK), BF16),
            pltpu.VMEM((rows, 2 * BLOCK), BF16),
            pltpu.VMEM((rows, BLOCK), F32),
            pltpu.VMEM((rows, BLOCK), F32),
            pltpu.VMEM((8, width), F32),
            pltpu.VMEM((8, width), F32),
            pltpu.VMEM((len(digits) + 1, 8, width), F32),
            pltpu.VMEM((len(digits), 3, 8, width), F32),
            pltpu.SemaphoreType.DMA,
            pltpu.SemaphoreType.DMA,
            pltpu.SemaphoreType.DMA((len(digits), 3)),
            pltpu.SemaphoreType.DMA((len(digits), 3)),
            pltpu.VMEM((n, 8, LANES), F32),
            pltpu.VMEM((8, LANES), F32),
            pltpu.VMEM((n - 1, 8, LANES), F32),
            pltpu.VMEM((16, conv_ch), BF16),
            pltpu.SemaphoreType.DMA((n - 1,)),
            pltpu.SemaphoreType.DMA((n - 1,)),
            pltpu.SemaphoreType.DMA,
            pltpu.SemaphoreType.DMA,
            pltpu.VMEM((rows + 8, conv_ch), F32),
            pltpu.VMEM(((1 + far) * rows, 2 * heads), BF16),
            pltpu.VMEM(half, F32),
            pltpu.VMEM((far,) + half, F32),
            pltpu.VMEM((2 * rows, 2 * heads), BF16),
            pltpu.VMEM((rows, 3 * heads), BF16),
            pltpu.VMEM((heads, rows), F32),
            pltpu.VMEM((2, rows, 2 * rows), F32),
            pltpu.VMEM((2, rows, 2 * rows), F32),
            pltpu.VMEM((2 * rows, 2 * rows), BF16),
            pltpu.VMEM((2 * rows, 2 * rows), BF16),
            pltpu.VMEM((rows, 2 * rows), F32),
            pltpu.VMEM(half, BF16),
            pltpu.VMEM(half, BF16),
            *[pltpu.VMEM(stack, BF16)] * 7,
            pltpu.VMEM(half, BF16),
            pltpu.VMEM(half, BF16),
            pltpu.SemaphoreType.DMA((5, far)),
            pltpu.SemaphoreType.DMA((5, far)),
            pltpu.VMEM(piece, F32),
            pltpu.VMEM(piece, F32),
        ],
        compiler_params=pltpu.CompilerParams(
            collective_id=0, has_side_effects=True, vmem_limit_bytes=VMEM_LIMIT
        ),
    )(conv_input, conv_weight, log_decay, level_weight, grad_out)


def solution(mesh):
    def body(*args):
        return travel(lax.axis_size("ctx"), *args)

    in_specs = (
        P(("groups", "ctx"), None),
        P(),
        P(None, ("groups", "ctx")),
        P(None, None, ("groups", "ctx")),
        P(("groups", "ctx"), None),
    )
    out_specs = (
        P(("groups", "ctx"), None),
        P(("groups", "ctx"), None),
        P(None, None, ("groups", "ctx")),
        P("groups", None),
    )
    return jax.shard_map(body, mesh=mesh, in_specs=in_specs, out_specs=out_specs, check_vma=False)
```
